256 devices in a mesh: ctx: 32 (over z_lo, x, core), dp: 8 (over z_hi, y).
Axes of the slice: x: 4, y: 4, z: 8 (z_hi: 2, z_lo: 4; z = z_hi * 4 + z_lo), core: 2. Of those that a mesh axis runs over, the one named last changes fastest.
Arguments:
- q_nope: bfloat16 [4096, 8192], P('ctx', 'dp'), may hold values from -6 to 6
- q_rope: bfloat16 [4096, 4096], P('ctx', 'dp'), may hold values from -400 to 400
- latent: bfloat16 [4096, 512], P('ctx'), may hold values from -6 to 6
- rope_key: bfloat16 [4096, 64], P('ctx'), may hold values from -6 to 6
- segment_ids: int32 [4096], P('ctx'), may hold values from 0 to 3, as said below
- w_uk: bfloat16 [64, 128, 512], P('dp', 'ctx'), may hold values from -0.5 to 0.5
- w_uv: bfloat16 [64, 512, 128], P('dp', 'ctx'), may hold values from -0.25 to 0.25
- w_out: bfloat16 [8192, 7168], P('dp', 'ctx'), may hold values from -0.0625 to 0.0625
Outputs:
- mixed: bfloat16 [4096, 7168], P('ctx', 'dp')
- log_sum: float32 [4096, 64], P('ctx', 'dp')
The draws below stay inside these ranges and needn't reach their ends.
Inputs may be any that keep to these rules, and one draw needn't show every extreme that they name: `segment_ids`: document numbers never fall along the positions and every number of 0 to 3 occurs; one document holds exactly 3072 positions, every other at least 1.
All inputs are finite; a program needn't handle non-finite values.
Results may differ from the reference program's by a relative error of at most 0.017.
Values may be sent and summed in bfloat16 or wider, within the bound.
No kernel may reach another device: no remote copies, remote signals or barrier semaphores. Data moves between devices by JAX's collectives and lax.ppermute only.
A program may use at most 128 MiB of HBM per device.

```python
import jax
import jax.numpy as jnp
from jax import lax

D = 7168
HEADS = 64
HEAD_DIM = 128
KV_RANK = 512
ROPE_DIM = 64
DOCS = 4
TOKENS = 4096


def rope_base(key):
    return jnp.clip(jax.random.normal(key, (TOKENS, ROPE_DIM), jnp.float32), -6.0, 6.0)


def draw_rope_key(key, part):
    base = rope_base(key)
    return base.astype(jnp.bfloat16)


def draw_q_rope(key, part):
    key = jax.random.fold_in(key, 7)
    fresh = jax.random.normal(key, (TOKENS, HEADS * ROPE_DIM), jnp.float32)
    return jnp.clip(fresh, -6.0, 6.0).astype(jnp.bfloat16)


def draw_segment_ids(key, part):
    key = jax.random.fold_in(key, 23)
    first_key, second_key, slot_key = jax.random.split(key, 3)
    longest = 3 * TOKENS // 4
    rest = TOKENS - longest
    first_cut = jax.random.randint(first_key, (), 1, rest - 1, jnp.int32)
    second_cut = jax.random.randint(second_key, (), first_cut + 1, rest, jnp.int32)
    shorts = jnp.stack([first_cut, second_cut - first_cut, rest - second_cut]).astype(jnp.int32)
    slot = jax.random.randint(slot_key, (), 0, DOCS, jnp.int32)
    order = jnp.arange(DOCS, dtype=jnp.int32)
    short_index = jnp.clip(order - (order > slot).astype(jnp.int32), 0, DOCS - 2)
    lengths = jnp.where(order == slot, jnp.int32(longest), shorts[short_index])
    ends = jnp.cumsum(lengths).astype(jnp.int32)
    places = jnp.arange(TOKENS, dtype=jnp.int32)
    return jnp.sum((places[:, None] >= ends[None, :DOCS - 1]).astype(jnp.int32), axis=1).astype(jnp.int32)


def level_of(own_key, dims, cuts, low, largest):
    def one(axis_at, blocks):
        steps = jax.random.uniform(jax.random.fold_in(jax.random.fold_in(own_key, 6), axis_at), (blocks,), jnp.float32, low / len(cuts), largest / len(cuts))
        return jnp.repeat(jnp.exp(steps), dims[axis_at] // blocks).reshape((-1,) + (1,) * (len(dims) - axis_at - 1))

    loudness = one(*cuts[0])
    for cut in cuts[1:]:
        loudness = loudness * one(*cut)
    return loudness


def bell_draw(key, extent, spread, limit, cuts=(), kind=jnp.bfloat16):
    values = spread * jax.random.normal(key, extent, jnp.float32)
    if cuts:
        values = values * level_of(key, extent, cuts, -0.22, 0.18)
    return jnp.clip(values, -limit, limit).astype(kind)


def setup_inputs(seed: int = 0) -> dict:
    arg_keys = jax.random.split(jax.random.key(seed), 9)
    q_nope = bell_draw(arg_keys[0], (TOKENS, HEADS * HEAD_DIM), 1.0, 6.0, ((0, 32), (1, 8)))
    q_rope = draw_q_rope(jax.random.fold_in(arg_keys[8], 71), 0)
    latent = bell_draw(arg_keys[2], (TOKENS, KV_RANK), 1.0, 6.0, ((0, 32),))
    rope_key = draw_rope_key(jax.random.fold_in(arg_keys[8], 71), 0)
    segment_ids = draw_segment_ids(jax.random.fold_in(arg_keys[8], 71), 0)
    w_uk = bell_draw(arg_keys[5], (HEADS, HEAD_DIM, KV_RANK), HEAD_DIM ** -0.5, 0.5, ((0, 8), (1, 32)))
    w_uv = bell_draw(arg_keys[6], (HEADS, KV_RANK, HEAD_DIM), KV_RANK ** -0.5, 0.25, ((0, 8), (1, 32)))
    w_out = bell_draw(arg_keys[7], (HEADS * HEAD_DIM, D), (HEADS * HEAD_DIM) ** -0.5, 0.0625, ((0, 8), (1, 32)))
    return {"q_nope": q_nope, "q_rope": q_rope, "latent": latent, "rope_key": rope_key, "segment_ids": segment_ids, "w_uk": w_uk, "w_uv": w_uv, "w_out": w_out}


def reference(q_nope, q_rope, latent, rope_key, segment_ids, w_uk, w_uv, w_out):
    scale = (HEAD_DIM + ROPE_DIM) ** -0.5
    queries = q_nope.reshape(TOKENS, HEADS, HEAD_DIM).astype(jnp.float32)
    query_latent = jnp.einsum("thk,hkr->htr", queries, w_uk.astype(jnp.float32)).astype(jnp.bfloat16)
    rotary = q_rope.reshape(TOKENS, HEADS, ROPE_DIM).transpose(1, 0, 2)
    places = jnp.arange(TOKENS, dtype=jnp.int32)
    visible = (places[None, :] <= places[:, None]) & (segment_ids[None, :] == segment_ids[:, None])

    def one_head(pair):
        query_head, rotary_head = pair
        score = jnp.dot(query_head, latent.T, preferred_element_type=jnp.float32)
        score = score + jnp.dot(rotary_head, rope_key.T, preferred_element_type=jnp.float32)
        score = score * scale
        peak = jnp.max(jnp.where(visible, score, -jnp.inf), axis=1)
        expon = jnp.where(visible, jnp.exp(score - peak[:, None]), 0.0)
        total = jnp.sum(expon, axis=1)
        summed = jnp.dot(expon.astype(jnp.bfloat16), latent, preferred_element_type=jnp.float32)
        attended = (summed / total[:, None]).astype(jnp.bfloat16)
        return attended, peak + jnp.log(total)

    attended, log_heads = lax.map(one_head, (query_latent, rotary))
    values = jnp.einsum("htr,hrk->thk", attended.astype(jnp.float32), w_uv.astype(jnp.float32))
    values = values.astype(jnp.bfloat16).reshape(TOKENS, HEADS * HEAD_DIM)
    mixed = jnp.dot(values, w_out, preferred_element_type=jnp.float32).astype(jnp.bfloat16)
    return mixed, log_heads.T
```

```python
import jax
import jax.numpy as jnp
from jax import lax
from jax.experimental import pallas as pl
from jax.experimental.pallas import tpu as pltpu
from jax.sharding import PartitionSpec as P

HEAD_DIM = 128
KV_RANK = 512
ROPE_DIM = 64
WIDE = 640
TILE = 512
CHUNK = 256
FAR = -1e30
LOG2E = 1.4426950408889634
SCALE = (HEAD_DIM + ROPE_DIM) ** (-0.5)
AXES = ("ctx", "dp")
MIB = 1024 * 1024
VMEM = pl.BlockSpec(memory_space=pltpu.VMEM)
SMEM = pl.BlockSpec(memory_space=pltpu.SMEM)
ANY = pl.BlockSpec(memory_space=pl.ANY)


def moved(array, to):
    pairs = []
    for ctx in range(32):
        for dp in range(8):
            z, x, core, half, y = to(ctx // 8, ctx // 2 % 4, ctx % 2, dp // 4, dp % 4)
            pairs.append((ctx * 8 + dp, (z * 8 + x * 2 + core) * 8 + half * 4 + y))
    return lax.ppermute(array, AXES, pairs)


def along_x(by):
    return lambda z, x, core, half, y: (z, (x + by) % 4, core, half, y)


def along_y(by):
    return lambda z, x, core, half, y: (z, x, core, half, (y + by) % 4)


def along_z_ring(by):
    def to(z, x, core, half, y):
        whole = (half * 4 + z + by) % 8
        return (whole % 4, x, core, whole // 4, y)

    return to


def flip_z(bit):
    return lambda z, x, core, half, y: (z ^ bit, x, core, half, y)


def other_core(z, x, core, half, y):
    return (z, x, 1 - core, half, y)


def settle(other_half, cross):
    def to(z, x, core, half, y):
        low = 1 - x % 2 if cross else x % 2
        return (z, y % 2 * 2 + low, core, 1 - half if other_half else half, y // 2 * 2 + x // 2)

    return to


def contract_last(left, right):
    return lax.dot_general(left, right, (((1,), (1,)), ((), ())), preferred_element_type=jnp.float32)


def call(kernel, outs, in_specs, scratch=(), limit=32, flops=0, name=None):
    return pl.pallas_call(
        kernel,
        out_shape=tuple(jax.ShapeDtypeStruct(*out) for out in outs),
        in_specs=in_specs,
        out_specs=tuple(VMEM for _ in outs),
        scratch_shapes=list(scratch),
        compiler_params=pltpu.CompilerParams(vmem_limit_bytes=limit * MIB),
        cost_estimate=pl.CostEstimate(flops=flops, bytes_accessed=3 * MIB, transcendentals=0),
        name=name,
    )


def doc_columns(docs):
    return jnp.transpose(jnp.broadcast_to(docs.astype(jnp.float32), (128, 128)))


def keys_kernel(latent, rope_key, docs, out):
    out[:, 0:KV_RANK] = latent[...]
    rope = jnp.transpose(rope_key[...].astype(jnp.float32))
    doc = doc_columns(docs[...])
    lane = lax.broadcasted_iota(jnp.int32, (128, 128), 1)
    place = (lane - ROPE_DIM).astype(jnp.float32)
    tail = jnp.where(place == doc, 1.0, jnp.where(lane == ROPE_DIM + 4, doc, 0.0))
    tail = jnp.where(lane < ROPE_DIM, jnp.concatenate([rope, rope], axis=1), tail)
    out[:, KV_RANK:WIDE] = tail.astype(jnp.bfloat16)


def queries_kernel(place, q_nope, q_rope, docs, mine, theirs, query, up_value, up_key):
    z, x, core = place[0], place[1], place[2]
    row = lax.broadcasted_iota(jnp.int32, (512, 1), 0)
    position = row % 128 // 4
    slot = ((position % 2) ^ core) * 16 + ((position // 2 % 4 - x) & 3) * 4 + ((position // 8) ^ z)
    wanted = slot * 16 + row // 128 * 4 + row % 4
    pick = (lax.broadcasted_iota(jnp.int32, (512, 512), 1) == wanted).astype(jnp.float32)
    pick = pick.astype(jnp.bfloat16)
    for h in range(0, 8, 2):
        both = [
            jnp.concatenate(
                [side[:, :, n].reshape(256, 128) for side in (mine, theirs)], axis=0
            )
            for n in (h, h + 1)
        ]
        ordered = jnp.dot(pick, jnp.concatenate(both, axis=1), preferred_element_type=jnp.float32)
        ordered = ordered.astype(jnp.bfloat16)
        for n in (0, 1):
            for j in range(4):
                up_key[h + n, :, j * 128 : j * 128 + 128] = ordered[
                    j * 128 : j * 128 + 128, n * 128 : n * 128 + 128
                ]
    for side, array in enumerate((mine, theirs)):
        for dx in range(4):
            for dz in range(4):
                at = (z ^ dz) * 8 + ((x + dx) & 3) * 2 + (core ^ side)
                up_value[:, pl.ds(pl.multiple_of(at * 16, 16), 16), :] = array[dx, dz, 8:16]
    doc = doc_columns(docs[...])
    lane = lax.broadcasted_iota(jnp.int32, (128, 128), 1)
    other_doc = (lane >= ROPE_DIM) & (lane < ROPE_DIM + 4)
    other_doc = other_doc & ((lane - ROPE_DIM).astype(jnp.float32) != doc)
    marks = jnp.where(other_doc, FAR, 0.0).astype(jnp.bfloat16)[:, ROPE_DIM:]
    for h in range(8):
        rows = pl.ds(h * 128, 128)
        latent_part = jnp.dot(
            q_nope[:, h * 128 : h * 128 + 128], up_key[h], preferred_element_type=jnp.float32
        )
        query[rows, 0:KV_RANK] = latent_part.astype(jnp.bfloat16)
        query[rows, KV_RANK:WIDE] = jnp.concatenate(
            [q_rope[:, h * 64 : h * 64 + 64], marks], axis=1
        )


def attention_kernel(place, query, up_value, *rest):
    pieces, (values, log_sum, keys, score, total, peak, weighed, sems) = rest[:16], rest[16:]
    z, x, core = place[0], place[1], place[2]
    copies = []
    for side in range(2):
        for dz in range(4):
            for dx in range(4):
                source = pieces[side * 8 + dz * 2 + dx // 2]
                block = (((z + dz) & 3) * 4 + ((x + dx) & 3)) * 2 + (core ^ side)
                copies.append(
                    pltpu.make_async_copy(
                        source.at[dx % 2],
                        keys.at[pl.ds(pl.multiple_of(block * 128, 128), 128)],
                        sems.at[len(copies)],
                    )
                )
    for copy in copies:
        copy.start()
    for copy in copies:
        copy.wait()

    lane = lax.broadcasted_iota(jnp.int32, (16, 128), 1)
    own_tile = lax.div(place[3], TILE // 128)
    low = jnp.int32(0)
    for tile in range(4096 // TILE):
        last = keys[tile * TILE + TILE - 16 : tile * TILE + TILE, KV_RANK:WIDE].astype(jnp.float32)
        doc = jnp.max(jnp.where(lane == ROPE_DIM + 4, last, -1.0)).astype(jnp.int32)
        low = low + jnp.where(doc < place[4], 1, 0)

    def lane_groups(array, join):
        parts = [array[:, n * 128 : n * 128 + 128] for n in range(TILE // 128)]
        return join(join(parts[0], parts[1]), join(parts[2], parts[3]))

    def scores(tile, first):
        start = pl.multiple_of(tile * TILE, TILE)
        for part in range(1024 // CHUNK):
            rows = pl.ds(part * CHUNK, CHUNK)
            new = contract_last(query[rows, :], keys[pl.ds(start, TILE), :])
            if first:
                at = lax.broadcasted_iota(jnp.int32, (CHUNK, TILE), 0)
                row_place = place[3] * 128 + (at & 127)
                key_place = start + lax.broadcasted_iota(jnp.int32, (CHUNK, TILE), 1)
                new = jnp.where(key_place <= row_place, new, FAR)
            score[tile, rows, :] = new
            best = lane_groups(new, jnp.maximum)
            peak[rows, :] = best if first else jnp.maximum(peak[rows, :], best)

    def weigh(tile, first):
        start = pl.multiple_of(tile * TILE, TILE)
        for part in range(1024 // CHUNK):
            rows = pl.ds(part * CHUNK, CHUNK)
            top = peak[rows, :]
            top = jnp.concatenate([top] * (TILE // 128), axis=1)
            expon = jnp.exp2((score[tile, rows, :] - top) * (SCALE * LOG2E))
            lanes = lane_groups(expon, jnp.add)
            product = jnp.dot(
                expon.astype(jnp.bfloat16),
                keys[pl.ds(start, TILE), 0:KV_RANK],
                preferred_element_type=jnp.float32,
            )
            total[rows, :] = lanes if first else total[rows, :] + lanes
            weighed[rows, :] = product if first else weighed[rows, :] + product

    def each(do):
        do(own_tile, True)
        lax.fori_loop(low, own_tile, lambda tile, carry: (do(tile, False), carry)[1], 0)

    each(scores)
    for part in range(1024 // CHUNK):
        rows = pl.ds(part * CHUNK, CHUNK)
        top = jnp.max(peak[rows, :], axis=1, keepdims=True)
        peak[rows, :] = jnp.broadcast_to(top, (CHUNK, 128))
    each(weigh)

    column = lax.broadcasted_iota(jnp.int32, (128, 128), 1)
    logs = jnp.zeros((128, 128), jnp.float32)
    for h in range(8):
        rows = pl.ds(h * 128, 128)
        whole = jnp.sum(total[rows, :], axis=1, keepdims=True)
        attended = (weighed[rows, :] / whole).astype(jnp.bfloat16)
        value = jnp.dot(attended, up_value[h], preferred_element_type=jnp.float32)
        values[h * 128 : h * 128 + 128, :] = jnp.transpose(value).astype(jnp.bfloat16)
        logs = jnp.where(column == h, peak[rows, :] * SCALE + jnp.log(whole), logs)
    log_sum[...] = jnp.transpose(logs)[0:8, :]


def project_kernel(count, place, *rest):
    gathered, mine, theirs, outs = rest[:4], rest[4], rest[5], rest[6 : 6 + 2 * count]
    values, weights, sems = rest[6 + 2 * count :]
    copies = []
    needed = 2 if count == 1 else 4
    for side, array in enumerate((mine, theirs)):
        for n in range(needed):
            block = 2 * n + lax.div(place[1], 2) if count == 1 else n
            copies.append(
                pltpu.make_async_copy(
                    array.at[block], weights.at[side, n], sems.at[side * needed + n]
                )
            )
    for copy in copies:
        copy.start()
    for dx in range(4):
        values[(place[0] + dx) & 3] = gathered[dx][...]
    for copy in copies:
        copy.wait()
    for n in range(count):
        which = place[1 + n]
        high, low = lax.div(which, 2), which & 1
        right = jnp.concatenate([values[2 * low], values[2 * low + 1]], axis=1)
        for half in range(2):
            for side in range(2):
                weight = weights[side, half if count == 1 else 2 * half + high]
                term = jnp.dot(weight, right, preferred_element_type=jnp.float32)
                term = term.astype(jnp.bfloat16)
                outs[2 * n + half][0, side] = term[:, 0:128]
                outs[2 * n + half][1, side] = term[:, 128:256]


def project(gathered, mine, theirs, x, which):
    count = len(which)
    needed = 2 if count == 1 else 4
    return call(
        lambda *refs: project_kernel(count, *refs),
        [((2, 2, 224, 128), jnp.bfloat16)] * (2 * count),
        [SMEM] + [VMEM] * 4 + [ANY] * 2,
        [
            pltpu.VMEM((4, 1024, 128), jnp.bfloat16),
            pltpu.VMEM((2, needed, 224, 1024), jnp.bfloat16),
            pltpu.SemaphoreType.DMA((2 * needed,)),
        ],
        flops=470_000_000 * count,
        name="project",
    )(jnp.stack([x] + which).astype(jnp.int32), *gathered, mine, theirs)


def sum_kernel(place, *rest):
    arrays, outs, summed = rest[:6], rest[6:10], rest[10]
    for half in range(2):
        own, left, right = arrays[3 * half : 3 * half + 3]
        for low in range(2):
            whole = own[low].astype(jnp.float32) + left[low].astype(jnp.float32)
            whole = whole + right[low].astype(jnp.float32)
            summed[half * 2 + low] = whole.astype(jnp.bfloat16)
    for n in range(4):
        outs[n][...] = summed[(place[0] ^ (n // 2)) * 2 + (place[1] ^ (n % 2))]


def finish_kernel(place, keep_same, keep_cross, give_same, give_cross, mixed, whole):
    low, core = place[0], place[1]
    for cross, pair in enumerate(((keep_same, give_same), (keep_cross, give_cross))):
        for side in range(2):
            term = pair[0][side].astype(jnp.float32) + pair[1][side].astype(jnp.float32)
            whole[(low ^ cross) * 2 + (core ^ side)] = term
    mixed[...] = jnp.transpose(whole[...].reshape(896, 128)).astype(jnp.bfloat16)


def gather_ring(block):
    return [block] + [moved(block, along_x(-by)) for by in (1, 2, 3)]


def per_device(q_nope, q_rope, latent, rope_key, segment_ids, w_uk, w_uv, w_out):
    ctx, dp = lax.axis_index("ctx"), lax.axis_index("dp")
    z, x, core = ctx // 8, ctx // 2 % 4, ctx % 2
    half, y = dp // 4, dp % 4
    place = jnp.stack([z, x, core, ctx, segment_ids[0]]).astype(jnp.int32)
    docs = segment_ids.reshape(1, 128)

    groups = [[zz * 8 + rest for zz in range(4)] for rest in range(8)]
    mine = lax.all_gather(w_out.T, "ctx", axis=0, axis_index_groups=groups)
    theirs = moved(mine, other_core)

    (block,) = call(
        keys_kernel, [((128, WIDE), jnp.bfloat16)], [VMEM] * 3, name="keys"
    )(latent, rope_key.T, docs)
    ring = gather_ring(block)
    here = [jnp.stack(ring[:2]), jnp.stack(ring[2:])]
    plus = [moved(part, along_z_ring(-1)) for part in here]
    minus = [moved(part, along_z_ring(1)) for part in here]
    two = [moved(plus[0], along_z_ring(-1)), moved(minus[1], along_z_ring(1))]
    pieces = here + plus + two + minus
    pieces = pieces + [moved(piece, other_core) for piece in pieces]

    up = w_uk.reshape(8, 4, 4, 128).transpose(0, 2, 1, 3).reshape(8, 16, 128)
    up = jnp.concatenate([up, w_uv])
    up = jnp.stack([up, moved(up, flip_z(1))])
    up = jnp.stack([up, moved(up, flip_z(2))])
    up = jnp.stack(gather_ring(up.reshape(4, 16, 16, 128)))
    query, up_value = call(
        queries_kernel,
        [((1024, WIDE), jnp.bfloat16), ((8, KV_RANK, HEAD_DIM), jnp.bfloat16)],
        [SMEM] + [VMEM] * 5,
        [pltpu.VMEM((8, HEAD_DIM, KV_RANK), jnp.bfloat16)],
        flops=700_000_000,
        name="queries",
    )(place, q_nope, q_rope, docs, up, moved(up, other_core))

    values, log_sum = call(
        attention_kernel,
        [((1024, 128), jnp.bfloat16), ((8, 128), jnp.float32)],
        [SMEM, VMEM, VMEM] + [ANY] * 16,
        [
            pltpu.VMEM((4096, WIDE), jnp.bfloat16),
            pltpu.VMEM((4096 // TILE, 1024, TILE), jnp.float32),
            pltpu.VMEM((1024, 128), jnp.float32),
            pltpu.VMEM((1024, 128), jnp.float32),
            pltpu.VMEM((1024, KV_RANK), jnp.float32),
            pltpu.SemaphoreType.DMA((32,)),
        ],
        limit=48,
        flops=10_000_000_000,
        name="attention",
    )(place, query, up_value, *pieces)

    gathered = gather_ring(values)
    far = project(gathered, mine, theirs, x, [(y + 2) % 4])
    far = moved(far[0], along_y(1)), moved(far[1], along_y(-1))
    terms = project(gathered, mine, theirs, x, [(y + 1) % 4, (y + 3) % 4, y])
    right, left, own = terms[0:2], terms[2:4], terms[4:6]
    from_left = [moved(right[0] + far[0], along_y(1)), moved(right[1], along_y(1))]
    from_right = [moved(left[0], along_y(-1)), moved(left[1] + far[1], along_y(-1))]
    sums = call(
        sum_kernel,
        [((2, 224, 128), jnp.bfloat16)] * 4,
        [SMEM] + [VMEM] * 6,
        [pltpu.VMEM((4, 2, 224, 128), jnp.bfloat16)],
        name="sums",
    )(
        jnp.stack([half, x % 2]).astype(jnp.int32),
        own[0], from_left[0], from_right[0], own[1], from_left[1], from_right[1],
    )
    sums = [moved(term, settle(n // 2, n % 2)) for n, term in enumerate(sums)]
    (mixed,) = call(
        finish_kernel,
        [((128, 896), jnp.bfloat16)],
        [SMEM] + [VMEM] * 4,
        [pltpu.VMEM((4, 224, 128), jnp.float32)],
        name="finish",
    )(jnp.stack([x % 2, core]).astype(jnp.int32), *sums)
    return (mixed, log_sum.T)


def solution(mesh):
    return jax.shard_map(
        per_device,
        mesh=mesh,
        in_specs=(
            P("ctx", "dp"),
            P("ctx", "dp"),
            P("ctx", None),
            P("ctx", None),
            P("ctx"),
            P("dp", "ctx", None),
            P("dp", "ctx", None),
            P("dp", "ctx"),
        ),
        out_specs=(P("ctx", "dp"), P("ctx", "dp")),
        check_vma=False,
    )
```

```python
import jax
import jax.numpy as jnp
from jax import lax
from jax.experimental import pallas as pl
from jax.experimental.pallas import tpu as pltpu
from jax.sharding import PartitionSpec as P

HEAD_DIM = 128
KV_RANK = 512
ROPE_DIM = 64
WIDE = 640
TILE = 512
CHUNK = 256
FAR = -1e30
LOG2E = 1.4426950408889634
SCALE = (HEAD_DIM + ROPE_DIM) ** (-0.5)
AXES = ("ctx", "dp")
MIB = 1024 * 1024
VMEM = pl.BlockSpec(memory_space=pltpu.VMEM)
SMEM = pl.BlockSpec(memory_space=pltpu.SMEM)
ANY = pl.BlockSpec(memory_space=pl.ANY)
HBM = pl.BlockSpec(memory_space=pltpu.HBM)


def moved(array, to):
    pairs = []
    for ctx in range(32):
        for dp in range(8):
            z, x, core, half, y = to(ctx // 8, ctx // 2 % 4, ctx % 2, dp // 4, dp % 4)
            pairs.append((ctx * 8 + dp, (z * 8 + x * 2 + core) * 8 + half * 4 + y))
    return lax.ppermute(array, AXES, pairs)


def along_x(by):
    return lambda z, x, core, half, y: (z, (x + by) % 4, core, half, y)


def along_y(by):
    return lambda z, x, core, half, y: (z, x, core, half, (y + by) % 4)


def along_z_ring(by):
    def to(z, x, core, half, y):
        whole = (half * 4 + z + by) % 8
        return (whole % 4, x, core, whole // 4, y)

    return to


def flip_z(bit):
    return lambda z, x, core, half, y: (z ^ bit, x, core, half, y)


def other_core(z, x, core, half, y):
    return (z, x, 1 - core, half, y)


def other_half(z, x, core, half, y):
    return (z, x, core, 1 - half, y)


def settle(cross, swap):
    def to(z, x, core, half, y):
        low = 1 - x % 2 if cross else x % 2
        return (z, y % 2 * 2 + low, 1 - core if swap else core, half, y // 2 * 2 + x // 2)

    return to


def contract_last(left, right):
    return lax.dot_general(left, right, (((1,), (1,)), ((), ())), preferred_element_type=jnp.float32)


def call(kernel, outs, in_specs, scratch=(), limit=32, flops=0, name=None):
    return pl.pallas_call(
        kernel,
        out_shape=tuple(jax.ShapeDtypeStruct(*out) for out in outs),
        in_specs=in_specs,
        out_specs=tuple(VMEM for _ in outs),
        scratch_shapes=list(scratch),
        compiler_params=pltpu.CompilerParams(vmem_limit_bytes=limit * MIB),
        cost_estimate=pl.CostEstimate(flops=flops, bytes_accessed=3 * MIB, transcendentals=0),
        name=name,
    )


def doc_columns(docs):
    return jnp.transpose(jnp.broadcast_to(docs.astype(jnp.float32), (128, 128)))


def fetched(pairs, sems):
    copies = [pltpu.make_async_copy(a, b, sems.at[n]) for n, (a, b) in enumerate(pairs)]
    for copy in copies:
        copy.start()
    return copies


def keys_kernel(latent_in, rope_in, docs_in, out, rope_key, docs, sems):
    copies = fetched(
        [(latent_in, out.at[:, 0:KV_RANK]), (rope_in, rope_key), (docs_in, docs)], sems
    )
    for copy in copies:
        copy.wait()
    rope = jnp.transpose(rope_key[...].astype(jnp.float32))
    doc = doc_columns(docs[...])
    lane = lax.broadcasted_iota(jnp.int32, (128, 128), 1)
    place = (lane - ROPE_DIM).astype(jnp.float32)
    tail = jnp.where(place == doc, 1.0, jnp.where(lane == ROPE_DIM + 4, doc, 0.0))
    tail = jnp.where(lane < ROPE_DIM, jnp.concatenate([rope, rope], axis=1), tail)
    out[:, KV_RANK:WIDE] = tail.astype(jnp.bfloat16)


def first_kernel(*refs):
    row, line = refs[-2:]
    for n in range(4):
        row[n] = refs[n][...]
        line[n] = refs[4 + n][...]


def second_kernel(row, plus, minus, *rest):
    ring, (low, high, twelve, ups) = rest[:4], rest[4:]
    low[...] = plus[0:2]
    high[...] = minus[2:4]
    for n, part in enumerate((row, plus, minus)):
        twelve[4 * n : 4 * n + 4] = part[...]
    for n in range(4):
        ups[n] = ring[n][...]


def gate_kernel(weight_in, low_in, high_in, token, weight, low, high, sems):
    copies = fetched([(weight_in, weight)], sems)
    low[...] = low_in[...]
    high[...] = high_in[...]
    for copy in copies:
        copy.wait()


def hold_kernel(values_in, weight_in, first, second, values, weight):
    values[...] = values_in[...]
    weight[...] = weight_in[...]


def queries_kernel(
    place, q_nope_in, q_rope_in, docs, mine, theirs, query, up_value, token, up_key, q_nope, q_rope, sems
):
    token[...] = jnp.zeros((8, 128), jnp.float32)
    copies = fetched([(q_nope_in, q_nope), (q_rope_in, q_rope)], sems)
    z, x, core = place[0], place[1], place[2]
    row = lax.broadcasted_iota(jnp.int32, (512, 1), 0)
    position = row % 128 // 4
    slot = ((position % 2) ^ core) * 16 + ((position // 2 % 4 - x) & 3) * 4 + ((position // 8) ^ z)
    wanted = slot * 16 + row // 128 * 4 + row % 4
    pick = (lax.broadcasted_iota(jnp.int32, (512, 512), 1) == wanted).astype(jnp.float32)
    pick = pick.astype(jnp.bfloat16)
    for h in range(0, 8, 2):
        both = [
            jnp.concatenate(
                [side[:, :, n].reshape(256, 128) for side in (mine, theirs)], axis=0
            )
            for n in (h, h + 1)
        ]
        ordered = jnp.dot(pick, jnp.concatenate(both, axis=1), preferred_element_type=jnp.float32)
        ordered = ordered.astype(jnp.bfloat16)
        for n in (0, 1):
            for j in range(4):
                up_key[h + n, :, j * 128 : j * 128 + 128] = ordered[
                    j * 128 : j * 128 + 128, n * 128 : n * 128 + 128
                ]
    for side, array in enumerate((mine, theirs)):
        for dx in range(4):
            for dz in range(4):
                at = (z ^ dz) * 8 + ((x + dx) & 3) * 2 + (core ^ side)
                up_value[:, pl.ds(pl.multiple_of(at * 16, 16), 16), :] = array[dx, dz, 8:16]
    doc = doc_columns(docs[...])
    lane = lax.broadcasted_iota(jnp.int32, (128, 128), 1)
    other_doc = (lane >= ROPE_DIM) & (lane < ROPE_DIM + 4)
    other_doc = other_doc & ((lane - ROPE_DIM).astype(jnp.float32) != doc)
    marks = jnp.where(other_doc, FAR, 0.0).astype(jnp.bfloat16)[:, ROPE_DIM:]
    for copy in copies:
        copy.wait()
    for h in range(8):
        rows = pl.ds(h * 128, 128)
        latent_part = jnp.dot(
            q_nope[:, h * 128 : h * 128 + 128], up_key[h], preferred_element_type=jnp.float32
        )
        query[rows, 0:KV_RANK] = latent_part.astype(jnp.bfloat16)
        query[rows, KV_RANK:WIDE] = jnp.concatenate(
            [q_rope[:, h * 64 : h * 64 + 64], marks], axis=1
        )


def attention_kernel(place, query, up_value, *rest):
    pieces, (values, log_sum, keys, score, total, peak, weighed, sems) = rest[:6], rest[6:]
    z, x, core = place[0], place[1], place[2]
    blocks = TILE // 128
    own_tile = lax.div(place[3], blocks)

    def copy_of(source, block):
        rows = pl.ds(pl.multiple_of(block * 128, 128), 128)
        return pltpu.make_async_copy(source, keys.at[rows], sems.at[block])

    for side in range(2):
        twelve, two_low, two_high = pieces[side * 3 : side * 3 + 3]
        for dz, dx in [(a, b) for a in range(4) for b in range(4)]:
            if dz == 2:
                source = two_low.at[dx] if dx < 2 else two_high.at[dx - 2]
            else:
                source = twelve.at[{0: 0, 1: 4, 3: 8}[dz] + dx]
            block = (((z + dz) & 3) * 4 + ((x + dx) & 3)) * 2 + (core ^ side)

            @pl.when(block < (own_tile + 1) * blocks)
            def _():
                copy_of(source, block).start()

    def arrived(block):
        copy_of(pieces[0].at[0], block).wait()

    for n in range(blocks):
        arrived(own_tile * blocks + n)

    def lane_groups(array, join):
        parts = [array[:, n * 128 : n * 128 + 128] for n in range(TILE // 128)]
        return join(join(parts[0], parts[1]), join(parts[2], parts[3]))

    def scores(tile, first):
        start = pl.multiple_of(tile * TILE, TILE)
        for part in range(1024 // CHUNK):
            rows = pl.ds(part * CHUNK, CHUNK)
            new = contract_last(query[rows, :], keys[pl.ds(start, TILE), :])
            if first:
                at = lax.broadcasted_iota(jnp.int32, (CHUNK, TILE), 0)
                row_place = place[3] * 128 + (at & 127)
                key_place = start + lax.broadcasted_iota(jnp.int32, (CHUNK, TILE), 1)
                new = jnp.where(key_place <= row_place, new, FAR)
            score[tile, rows, :] = new
            best = lane_groups(new, jnp.maximum)
            peak[rows, :] = best if first else jnp.maximum(peak[rows, :], best)

    def weigh(tile, first):
        start = pl.multiple_of(tile * TILE, TILE)
        for part in range(1024 // CHUNK):
            rows = pl.ds(part * CHUNK, CHUNK)
            top = peak[rows, :]
            top = jnp.concatenate([top] * (TILE // 128), axis=1)
            expon = jnp.exp2((score[tile, rows, :] - top) * (SCALE * LOG2E))
            lanes = lane_groups(expon, jnp.add)
            product = jnp.dot(
                expon.astype(jnp.bfloat16),
                keys[pl.ds(start, TILE), 0:KV_RANK],
                preferred_element_type=jnp.float32,
            )
            total[rows, :] = lanes if first else total[rows, :] + lanes
            weighed[rows, :] = product if first else weighed[rows, :] + product

    def each_before(do):
        lax.fori_loop(low, own_tile, lambda tile, carry: (do(tile, False), carry)[1], 0)

    scores(own_tile, True)
    lax.fori_loop(0, own_tile * blocks, lambda block, carry: (arrived(block), carry)[1], 0)
    lane = lax.broadcasted_iota(jnp.int32, (16, 128), 1)
    row_at = lax.broadcasted_iota(jnp.int32, (16, 128), 0)
    earlier = jnp.zeros((16, 128), jnp.float32)
    for tile in range(4096 // TILE):
        last = keys[tile * TILE + TILE - 16 : tile * TILE + TILE, KV_RANK:WIDE].astype(jnp.float32)
        before = (last < place[4].astype(jnp.float32)) & (jnp.int32(tile) < own_tile)
        earlier = earlier + jnp.where(before, 1.0, 0.0)
    here = (lane == ROPE_DIM + 4) & (row_at == 15)
    low = jnp.max(jnp.where(here, earlier, 0.0)).astype(jnp.int32)
    each_before(scores)
    for part in range(1024 // CHUNK):
        rows = pl.ds(part * CHUNK, CHUNK)
        top = jnp.max(peak[rows, :], axis=1, keepdims=True)
        peak[rows, :] = jnp.broadcast_to(top, (CHUNK, 128))
    weigh(own_tile, True)
    each_before(weigh)

    column = lax.broadcasted_iota(jnp.int32, (128, 128), 1)
    logs = jnp.zeros((128, 128), jnp.float32)
    for h in range(8):
        rows = pl.ds(h * 128, 128)
        whole = jnp.sum(total[rows, :], axis=1, keepdims=True)
        attended = (weighed[rows, :] / whole).astype(jnp.bfloat16)
        value = jnp.dot(attended, up_value[h], preferred_element_type=jnp.float32)
        values[h * 128 : h * 128 + 128, :] = jnp.transpose(value).astype(jnp.bfloat16)
        logs = jnp.where(column == h, peak[rows, :] * SCALE + jnp.log(whole), logs)
    log_sum[...] = jnp.transpose(logs)[0:8, :]


def third_kernel(place, *refs):
    for dx in range(4):
        refs[5][(place[0] + dx) & 3] = refs[dx][...]


def project_kernel(place, mine, theirs, *rest):
    blocks, outs, (weights, sems) = rest[:4], rest[4:12], rest[12:]
    copies = []
    for dz in range(4):
        at = place[0] ^ dz
        copies.append((blocks[dz], weights.at[at & 1, 1 - (lax.div(at, 2) ^ place[5])]))
    copies = fetched(copies, sems)
    for copy in copies:
        copy.wait()
    for n in range(4):
        which = place[1 + n]
        high, low = lax.div(which, 2), which & 1
        right = jnp.concatenate(
            [mine[2 * low], theirs[2 * low], mine[2 * low + 1], theirs[2 * low + 1]], axis=1
        )
        weight = weights[high].reshape(448, 1024)
        terms = jnp.dot(weight, right, preferred_element_type=jnp.float32).astype(jnp.bfloat16)
        for half in range(2):
            for at in range(2):
                outs[2 * n + half][at] = terms[
                    half * 224 : half * 224 + 224, at * 256 : at * 256 + 256
                ]


def sum_kernel(own, left, right, out):
    whole = own[...].astype(jnp.float32) + left[...].astype(jnp.float32)
    out[...] = (whole + right[...].astype(jnp.float32)).astype(jnp.bfloat16)


def settle_kernel(place, own, left, right, arrived, *rest):
    outs, summed = rest[:4], rest[4]
    whole = own[...].astype(jnp.float32) + left[...].astype(jnp.float32)
    whole = whole + right[...].astype(jnp.float32) + arrived[...].astype(jnp.float32)
    summed[...] = whole.astype(jnp.bfloat16)
    for n in range(4):
        outs[n][...] = summed[place[0] ^ (n // 2), :, n % 2 * 128 : n % 2 * 128 + 128]


def finish_kernel(place, *rest):
    arrays, (mixed, whole) = rest[:4], rest[4:]
    for n in range(4):
        at = (place[0] ^ (n // 2)) * 2 + (place[1] ^ (n % 2))
        whole[at] = arrays[n][...].astype(jnp.float32)
    mixed[...] = jnp.transpose(whole[...].reshape(896, 128)).astype(jnp.bfloat16)


def gather_ring(block):
    return [block] + [moved(block, along_x(-by)) for by in (1, 2, 3)]


def per_device(q_nope, q_rope, latent, rope_key, segment_ids, w_uk, w_uv, w_out):
    ctx, dp = lax.axis_index("ctx"), lax.axis_index("dp")
    z, x, core = ctx // 8, ctx // 2 % 4, ctx % 2
    half, y = dp // 4, dp % 4
    place = jnp.stack([z, x, core, ctx, segment_ids[0]]).astype(jnp.int32)
    docs = segment_ids.reshape(1, 128)

    (block,) = call(
        keys_kernel,
        [((128, WIDE), jnp.bfloat16)],
        [HBM] * 3,
        [
            pltpu.VMEM((ROPE_DIM, 128), jnp.bfloat16),
            pltpu.VMEM((1, 128), jnp.int32),
            pltpu.SemaphoreType.DMA((3,)),
        ],
        limit=8,
        name="keys",
    )(latent, rope_key.T, docs)
    up = w_uk.reshape(8, 4, 4, 128).transpose(0, 2, 1, 3).reshape(8, 16, 128)
    up = jnp.concatenate([up, w_uv])
    ring = gather_ring(block)
    line = [up] + [moved(up, flip_z(bits)) for bits in (1, 2, 3)]
    row, line = call(
        first_kernel,
        [((4, 128, WIDE), jnp.bfloat16), ((4, 16, 16, 128), jnp.bfloat16)],
        [VMEM] * 8,
        limit=16,
        name="first",
    )(*ring, *line)
    plus, minus = moved(row, along_z_ring(-1)), moved(row, along_z_ring(1))
    low, high, twelve, ups = call(
        second_kernel,
        [
            ((2, 128, WIDE), jnp.bfloat16),
            ((2, 128, WIDE), jnp.bfloat16),
            ((12, 128, WIDE), jnp.bfloat16),
            ((4, 4, 16, 16, 128), jnp.bfloat16),
        ],
        [VMEM] * 7,
        limit=16,
        name="second",
    )(row, plus, minus, *gather_ring(line))
    pieces = [twelve, moved(low, along_z_ring(-1)), moved(high, along_z_ring(1))]
    theirs = moved(twelve, other_core)

    query, up_value, token = call(
        queries_kernel,
        [
            ((1024, WIDE), jnp.bfloat16),
            ((8, KV_RANK, HEAD_DIM), jnp.bfloat16),
            ((8, 128), jnp.float32),
        ],
        [SMEM] + [HBM] * 2 + [VMEM] * 3,
        [
            pltpu.VMEM((8, HEAD_DIM, KV_RANK), jnp.bfloat16),
            pltpu.VMEM((128, 1024), jnp.bfloat16),
            pltpu.VMEM((128, 512), jnp.bfloat16),
            pltpu.SemaphoreType.DMA((2,)),
        ],
        limit=16,
        flops=700_000_000,
        name="queries",
    )(place, q_nope, q_rope, docs, ups, moved(ups, other_core))

    weight, low, high = call(
        gate_kernel,
        [((224, 1024), jnp.bfloat16)] + [((2, 128, WIDE), jnp.bfloat16)] * 2,
        [HBM] + [VMEM] * 3,
        [pltpu.SemaphoreType.DMA((1,))],
        limit=8,
        name="gate",
    )(w_out.T, *pieces[1:], token)
    weights = [weight, moved(weight, flip_z(1)), moved(weight, flip_z(2))]
    pieces = [twelve, low, high, theirs, moved(low, other_core), moved(high, other_core)]
    values, log_sum = call(
        attention_kernel,
        [((1024, 128), jnp.bfloat16), ((8, 128), jnp.float32)],
        [SMEM, VMEM, VMEM] + [ANY] * 6,
        [
            pltpu.VMEM((4096, WIDE), jnp.bfloat16),
            pltpu.VMEM((4096 // TILE, 1024, TILE), jnp.float32),
            pltpu.VMEM((1024, 128), jnp.float32),
            pltpu.VMEM((1024, 128), jnp.float32),
            pltpu.VMEM((1024, KV_RANK), jnp.float32),
            pltpu.SemaphoreType.DMA((32,)),
        ],
        limit=32,
        flops=10_000_000_000,
        name="attention",
    )(place, query, up_value, *pieces)

    values, weight = call(
        hold_kernel,
        [((1024, 128), jnp.bfloat16), ((224, 1024), jnp.bfloat16)],
        [VMEM] * 4,
        limit=8,
        name="hold",
    )(values, *weights)
    weights.append(moved(weight, flip_z(3)))
    (gathered,) = call(
        third_kernel, [((4, 1024, 128), jnp.bfloat16)], [SMEM] + [VMEM] * 5, limit=8, name="third"
    )(x.reshape(1).astype(jnp.int32), *gather_ring(values), weights[3])
    order = [z, (y + 2) % 4, (y + 1) % 4, (y + 3) % 4, y, half]
    terms = call(
        project_kernel,
        [((2, 224, 256), jnp.bfloat16)] * 8,
        [SMEM] + [VMEM] * 2 + [ANY] * 4,
        [pltpu.VMEM((2, 2, 224, 1024), jnp.bfloat16), pltpu.SemaphoreType.DMA((4,))],
        limit=24,
        flops=1_880_000_000,
        name="project",
    )(jnp.stack(order).astype(jnp.int32), gathered, moved(gathered, other_core), *weights)
    far, right, left, own = terms[0:2], terms[2:4], terms[4:6], terms[6:8]
    far = moved(far[0], along_y(1)), moved(far[1], along_y(-1))
    from_left = [moved(right[0] + far[0], along_y(1)), moved(right[1], along_y(1))]
    from_right = [moved(left[0], along_y(-1)), moved(left[1] + far[1], along_y(-1))]
    (give,) = call(
        sum_kernel, [((2, 224, 256), jnp.bfloat16)], [VMEM] * 3, limit=16, name="sums"
    )(own[0], from_left[0], from_right[0])
    arrived = moved(give, other_half)
    low = jnp.stack([x % 2, core]).astype(jnp.int32)
    sums = call(
        settle_kernel,
        [((224, 128), jnp.bfloat16)] * 4,
        [SMEM] + [VMEM] * 4,
        [pltpu.VMEM((2, 224, 256), jnp.bfloat16)],
        limit=16,
        name="settle",
    )(low, own[1], from_left[1], from_right[1], arrived)
    (mixed,) = call(
        finish_kernel,
        [((128, 896), jnp.bfloat16)],
        [SMEM] + [VMEM] * 4,
        [pltpu.VMEM((4, 224, 128), jnp.float32)],
        limit=16,
        name="finish",
    )(low, *[moved(term, settle(n // 2, n % 2)) for n, term in enumerate(sums)])
    return (mixed, log_sum.T)


def solution(mesh):
    return jax.shard_map(
        per_device,
        mesh=mesh,
        in_specs=(
            P("ctx", "dp"),
            P("ctx", "dp"),
            P("ctx", None),
            P("ctx", None),
            P("ctx"),
            P("dp", "ctx", None),
            P("dp", "ctx", None),
            P("dp", "ctx"),
        ),
        out_specs=(P("ctx", "dp"), P("ctx", "dp")),
        check_vma=False,
    )
```

```python
import jax
import jax.numpy as jnp
from jax import lax
from jax.experimental import pallas as pl
from jax.experimental.pallas import tpu as pltpu
from jax.sharding import PartitionSpec as P

HEAD_DIM = 128
KV_RANK = 512
ROPE_DIM = 64
WIDE = 640
TILE = 512
CHUNK = 256
FAR = -1e30
LOG2E = 1.4426950408889634
SCALE = (HEAD_DIM + ROPE_DIM) ** (-0.5)
AXES = ("ctx", "dp")
MIB = 1024 * 1024
VMEM = pl.BlockSpec(memory_space=pltpu.VMEM)
SMEM = pl.BlockSpec(memory_space=pltpu.SMEM)
ANY = pl.BlockSpec(memory_space=pl.ANY)
HBM = pl.BlockSpec(memory_space=pltpu.HBM)


def moved(array, to):
    pairs = []
    for ctx in range(32):
        for dp in range(8):
            z, x, core, half, y = to(ctx // 8, ctx // 2 % 4, ctx % 2, dp // 4, dp % 4)
            pairs.append((ctx * 8 + dp, (z * 8 + x * 2 + core) * 8 + half * 4 + y))
    return lax.ppermute(array, AXES, pairs)


def along_x(by):
    return lambda z, x, core, half, y: (z, (x + by) % 4, core, half, y)


def along_y(by):
    return lambda z, x, core, half, y: (z, x, core, half, (y + by) % 4)


def along_z_ring(by):
    def to(z, x, core, half, y):
        whole = (half * 4 + z + by) % 8
        return (whole % 4, x, core, whole // 4, y)

    return to


def flip_z(bit):
    return lambda z, x, core, half, y: (z ^ bit, x, core, half, y)


def other_core(z, x, core, half, y):
    return (z, x, 1 - core, half, y)


def settle(cross, over):
    def to(z, x, core, half, y):
        low = 1 - x % 2 if cross else x % 2
        return (z, y % 2 * 2 + low, core, 1 - half if over else half, y // 2 * 2 + x // 2)

    return to


def contract_last(left, right):
    return lax.dot_general(left, right, (((1,), (1,)), ((), ())), preferred_element_type=jnp.float32)


def call(kernel, outs, in_specs, scratch=(), limit=32, flops=0, name=None):
    return pl.pallas_call(
        kernel,
        out_shape=tuple(jax.ShapeDtypeStruct(*out) for out in outs),
        in_specs=in_specs,
        out_specs=tuple(VMEM for _ in outs),
        scratch_shapes=list(scratch),
        compiler_params=pltpu.CompilerParams(vmem_limit_bytes=limit * MIB),
        cost_estimate=pl.CostEstimate(flops=flops, bytes_accessed=3 * MIB, transcendentals=0),
        name=name,
    )


def doc_columns(docs):
    return jnp.transpose(jnp.broadcast_to(docs.astype(jnp.float32), (128, 128)))


def fetched(pairs, sems):
    copies = [pltpu.make_async_copy(a, b, sems.at[n]) for n, (a, b) in enumerate(pairs)]
    for copy in copies:
        copy.start()
    return copies


def keys_kernel(latent_in, rope_in, docs_in, out, rope_key, docs, sems):
    copies = fetched(
        [(latent_in, out.at[:, 0:KV_RANK]), (rope_in, rope_key), (docs_in, docs)], sems
    )
    for copy in copies:
        copy.wait()
    rope = jnp.transpose(rope_key[...].astype(jnp.float32))
    doc = doc_columns(docs[...])
    lane = lax.broadcasted_iota(jnp.int32, (128, 128), 1)
    place = (lane - ROPE_DIM).astype(jnp.float32)
    tail = jnp.where(place == doc, 1.0, jnp.where(lane == ROPE_DIM + 4, doc, 0.0))
    tail = jnp.where(lane < ROPE_DIM, jnp.concatenate([rope, rope], axis=1), tail)
    out[:, KV_RANK:WIDE] = tail.astype(jnp.bfloat16)


def first_kernel(*refs):
    row, line = refs[-2:]
    for n in range(4):
        row[n] = refs[n][...]
        line[n] = refs[4 + n][...]


def second_kernel(row, plus, minus, *rest):
    ring, (low, high, twelve, ups) = rest[:4], rest[4:]
    low[...] = plus[0:2]
    high[...] = minus[2:4]
    for n, part in enumerate((row, plus, minus)):
        twelve[4 * n : 4 * n + 4] = part[...]
    for n in range(4):
        ups[n] = ring[n][...]


def outer_kernel(right, left, low, high):
    low[...] = right[0:512]
    high[...] = left[512:1024]


def gate_kernel(low_in, high_in, token, low, high):
    low[...] = low_in[...]
    high[...] = high_in[...]


def hold_kernel(values_in, weight, values):
    values[...] = values_in[...]


def queries_kernel(place, q_nope_in, q_rope_in, weight_in, docs, mine, theirs, *rest):
    query, up_value, weight, token, up_key, q_nope, q_rope, sems = rest
    token[...] = jnp.zeros((8, 128), jnp.float32)
    copies = fetched([(q_nope_in, q_nope), (q_rope_in, q_rope), (weight_in, weight)], sems)
    z, x, core = place[0], place[1], place[2]
    row = lax.broadcasted_iota(jnp.int32, (512, 1), 0)
    position = row % 128 // 4
    slot = ((position % 2) ^ core) * 16 + ((position // 2 % 4 - x) & 3) * 4 + ((position // 8) ^ z)
    wanted = slot * 16 + row // 128 * 4 + row % 4
    pick = (lax.broadcasted_iota(jnp.int32, (512, 512), 1) == wanted).astype(jnp.float32)
    pick = pick.astype(jnp.bfloat16)
    for h in range(0, 8, 2):
        both = [
            jnp.concatenate(
                [side[:, :, n].reshape(256, 128) for side in (mine, theirs)], axis=0
            )
            for n in (h, h + 1)
        ]
        ordered = jnp.dot(pick, jnp.concatenate(both, axis=1), preferred_element_type=jnp.float32)
        ordered = ordered.astype(jnp.bfloat16)
        for n in (0, 1):
            for j in range(4):
                up_key[h + n, :, j * 128 : j * 128 + 128] = ordered[
                    j * 128 : j * 128 + 128, n * 128 : n * 128 + 128
                ]
    for side, array in enumerate((mine, theirs)):
        for dx in range(4):
            for dz in range(4):
                at = (z ^ dz) * 8 + ((x + dx) & 3) * 2 + (core ^ side)
                up_value[:, pl.ds(pl.multiple_of(at * 16, 16), 16), :] = array[dx, dz, 8:16]
    doc = doc_columns(docs[...])
    lane = lax.broadcasted_iota(jnp.int32, (128, 128), 1)
    other_doc = (lane >= ROPE_DIM) & (lane < ROPE_DIM + 4)
    other_doc = other_doc & ((lane - ROPE_DIM).astype(jnp.float32) != doc)
    marks = jnp.where(other_doc, FAR, 0.0).astype(jnp.bfloat16)[:, ROPE_DIM:]
    for copy in copies:
        copy.wait()
    for h in range(8):
        rows = pl.ds(h * 128, 128)
        latent_part = jnp.dot(
            q_nope[:, h * 128 : h * 128 + 128], up_key[h], preferred_element_type=jnp.float32
        )
        query[rows, 0:KV_RANK] = latent_part.astype(jnp.bfloat16)
        query[rows, KV_RANK:WIDE] = jnp.concatenate(
            [q_rope[:, h * 64 : h * 64 + 64], marks], axis=1
        )


def attention_kernel(place, query, up_value, *rest):
    pieces, (values, log_sum, keys, score, total, peak, weighed) = rest[:6], rest[6:]
    z, x, core = place[0], place[1], place[2]
    blocks = TILE // 128
    own_tile = lax.div(place[3], blocks)

    for side in range(2):
        twelve, two_low, two_high = pieces[side * 3 : side * 3 + 3]
        for dz, dx in [(a, b) for a in range(4) for b in range(4)]:
            block = (((z + dz) & 3) * 4 + ((x + dx) & 3)) * 2 + (core ^ side)

            @pl.when(block < (own_tile + 1) * blocks)
            def _():
                rows = pl.ds(pl.multiple_of(block * 128, 128), 128)
                if dz == 2:
                    keys[rows, :] = two_low[dx] if dx < 2 else two_high[dx - 2]
                else:
                    keys[rows, :] = twelve[{0: 0, 1: 4, 3: 8}[dz] + dx]

    def lane_groups(array, join):
        parts = [array[:, n * 128 : n * 128 + 128] for n in range(TILE // 128)]
        return join(join(parts[0], parts[1]), join(parts[2], parts[3]))

    def scores(tile, first):
        start = pl.multiple_of(tile * TILE, TILE)
        for part in range(1024 // CHUNK):
            rows = pl.ds(part * CHUNK, CHUNK)
            new = contract_last(query[rows, :], keys[pl.ds(start, TILE), :])
            if first:
                at = lax.broadcasted_iota(jnp.int32, (CHUNK, TILE), 0)
                row_place = place[3] * 128 + (at & 127)
                key_place = start + lax.broadcasted_iota(jnp.int32, (CHUNK, TILE), 1)
                new = jnp.where(key_place <= row_place, new, FAR)
            score[tile, rows, :] = new
            best = lane_groups(new, jnp.maximum)
            peak[rows, :] = best if first else jnp.maximum(peak[rows, :], best)

    def weigh(tile, first):
        start = pl.multiple_of(tile * TILE, TILE)
        for part in range(1024 // CHUNK):
            rows = pl.ds(part * CHUNK, CHUNK)
            top = peak[rows, :]
            top = jnp.concatenate([top] * (TILE // 128), axis=1)
            expon = jnp.exp2((score[tile, rows, :] - top) * (SCALE * LOG2E))
            lanes = lane_groups(expon, jnp.add)
            product = jnp.dot(
                expon.astype(jnp.bfloat16),
                keys[pl.ds(start, TILE), 0:KV_RANK],
                preferred_element_type=jnp.float32,
            )
            total[rows, :] = lanes if first else total[rows, :] + lanes
            weighed[rows, :] = product if first else weighed[rows, :] + product

    def each_before(do):
        lax.fori_loop(low, own_tile, lambda tile, carry: (do(tile, False), carry)[1], 0)

    scores(own_tile, True)
    lane = lax.broadcasted_iota(jnp.int32, (16, 128), 1)
    row_at = lax.broadcasted_iota(jnp.int32, (16, 128), 0)
    earlier = jnp.zeros((16, 128), jnp.float32)
    for tile in range(4096 // TILE):
        last = keys[tile * TILE + TILE - 16 : tile * TILE + TILE, KV_RANK:WIDE].astype(jnp.float32)
        before = (last < place[4].astype(jnp.float32)) & (jnp.int32(tile) < own_tile)
        earlier = earlier + jnp.where(before, 1.0, 0.0)
    here = (lane == ROPE_DIM + 4) & (row_at == 15)
    low = jnp.max(jnp.where(here, earlier, 0.0)).astype(jnp.int32)
    each_before(scores)
    for part in range(1024 // CHUNK):
        rows = pl.ds(part * CHUNK, CHUNK)
        top = jnp.max(peak[rows, :], axis=1, keepdims=True)
        peak[rows, :] = jnp.broadcast_to(top, (CHUNK, 128))
    weigh(own_tile, True)
    each_before(weigh)

    column = lax.broadcasted_iota(jnp.int32, (128, 128), 1)
    logs = jnp.zeros((128, 128), jnp.float32)
    for h in range(8):
        rows = pl.ds(h * 128, 128)
        whole = jnp.sum(total[rows, :], axis=1, keepdims=True)
        attended = (weighed[rows, :] * (1.0 / whole)).astype(jnp.bfloat16)
        value = jnp.dot(attended, up_value[h], preferred_element_type=jnp.float32)
        values[h * 128 : h * 128 + 128, :] = jnp.transpose(value).astype(jnp.bfloat16)
        logs = jnp.where(column == h, peak[rows, :] * SCALE + jnp.log(whole), logs)
    log_sum[...] = jnp.transpose(logs)[0:8, :]


def third_kernel(place, own, right, left, low, high, *rest):
    out = rest[-1]
    for dx, array in ((0, own), (1, right), (3, left)):
        out[(place[0] + dx) & 3] = array[...]
    out[(place[0] + 2) & 3, 0:512] = low[...]
    out[(place[0] + 2) & 3, 512:1024] = high[...]


def project_kernel(wanted, place, mine, theirs, weights, outs):
    for chip in sorted({chip for chip, _ in wanted}):
        high, low = lax.div(place[1 + chip], 2), place[1 + chip] & 1
        right = jnp.concatenate(
            [mine[2 * low], theirs[2 * low], mine[2 * low + 1], theirs[2 * low + 1]], axis=1
        )
        halves = [half for other, half in wanted if other == chip]
        weight = weights[high, halves[0] : halves[-1] + 1].reshape(224 * len(halves), 1024)
        terms = jnp.dot(weight, right, preferred_element_type=jnp.float32).astype(jnp.bfloat16)
        for n, half in enumerate(halves):
            out = outs[wanted.index((chip, half))]
            for low_bit in range(2):
                out[low_bit] = terms[
                    n * 224 : n * 224 + 224, low_bit * 256 : low_bit * 256 + 256
                ]


def first_terms_kernel(place, mine, theirs, *rest):
    blocks, (far_give, left_give, weights, sems) = rest[:4], rest[4:]
    copies = []
    for dz in range(4):
        at = place[0] ^ dz
        copies.append((blocks[dz], weights.at[at & 1, 1 - (lax.div(at, 2) ^ place[5])]))
    copies = fetched(copies, sems)
    for copy in copies:
        copy.wait()
    project_kernel([(0, 0), (2, 0)], place, mine, theirs, weights, [far_give, left_give])


def other_terms_kernel(place, mine, theirs, weights, out):
    wanted = [(0, 1), (1, 0), (1, 1), (2, 1), (3, 0), (3, 1)]
    project_kernel(wanted, place, mine, theirs, weights, [out.at[n] for n in range(6)])


def summed(*arrays):
    whole = arrays[0][...].astype(jnp.float32)
    for array in arrays[1:]:
        whole = whole + array[...].astype(jnp.float32)
    return whole.astype(jnp.bfloat16)


def early_kernel(terms, far_give, left_give, out, far_out):
    out[...] = summed(terms.at[1], far_give)
    far_out[...] = terms[0]


def give_kernel(place, terms, left, right, far_keep, *outs):
    same, cross, left_out, right_out, whole = outs
    whole[...] = summed(terms.at[4], left, right)
    same[...] = whole[place[0]]
    cross[...] = whole[1 - place[0]]
    left_out[...] = summed(terms.at[3], far_keep)
    right_out[...] = terms[2]


def keep_kernel(place, terms, left, right, same, cross, whole):
    whole[...] = summed(terms.at[5], left, right)
    same[...] = whole[place[0]]
    cross[...] = whole[1 - place[0]]


def halves_kernel(give_same, give_cross, keep_same, keep_cross, mine, theirs):
    for cross, pair in enumerate(((keep_same, give_same), (keep_cross, give_cross))):
        whole = summed(*pair)
        mine[cross] = whole[:, 0:128]
        theirs[cross] = whole[:, 128:256]


def finish_kernel(place, mine, theirs, mixed, whole):
    for cross in range(2):
        for side, array in enumerate((mine, theirs)):
            whole[(place[0] ^ cross) * 2 + (place[1] ^ side)] = array[cross].astype(jnp.float32)
    mixed[...] = jnp.transpose(whole[...].reshape(896, 128)).astype(jnp.bfloat16)


def gather_ring(block):
    return [block] + [moved(block, along_x(-by)) for by in (1, 2, 3)]


def per_device(q_nope, q_rope, latent, rope_key, segment_ids, w_uk, w_uv, w_out):
    ctx, dp = lax.axis_index("ctx"), lax.axis_index("dp")
    z, x, core = ctx // 8, ctx // 2 % 4, ctx % 2
    half, y = dp // 4, dp % 4
    place = jnp.stack([z, x, core, ctx, segment_ids[0]]).astype(jnp.int32)
    docs = segment_ids.reshape(1, 128)

    (block,) = call(
        keys_kernel,
        [((128, WIDE), jnp.bfloat16)],
        [HBM] * 3,
        [
            pltpu.VMEM((ROPE_DIM, 128), jnp.bfloat16),
            pltpu.VMEM((1, 128), jnp.int32),
            pltpu.SemaphoreType.DMA((3,)),
        ],
        limit=8,
        name="keys",
    )(latent, rope_key.T, docs)
    up = w_uk.reshape(8, 4, 4, 128).transpose(0, 2, 1, 3).reshape(8, 16, 128)
    up = jnp.concatenate([up, w_uv])
    ring = gather_ring(block)
    line = [up] + [moved(up, flip_z(bits)) for bits in (1, 2, 3)]
    row, line = call(
        first_kernel,
        [((4, 128, WIDE), jnp.bfloat16), ((4, 16, 16, 128), jnp.bfloat16)],
        [VMEM] * 8,
        limit=16,
        name="first",
    )(*ring, *line)
    plus, minus = moved(row, along_z_ring(-1)), moved(row, along_z_ring(1))
    low, high, twelve, ups = call(
        second_kernel,
        [
            ((2, 128, WIDE), jnp.bfloat16),
            ((2, 128, WIDE), jnp.bfloat16),
            ((12, 128, WIDE), jnp.bfloat16),
            ((4, 4, 16, 16, 128), jnp.bfloat16),
        ],
        [VMEM] * 7,
        limit=16,
        name="second",
    )(row, plus, minus, *gather_ring(line))
    pieces = [twelve, moved(low, along_z_ring(-1)), moved(high, along_z_ring(1))]
    theirs = moved(twelve, other_core)

    query, up_value, weight, token = call(
        queries_kernel,
        [
            ((1024, WIDE), jnp.bfloat16),
            ((8, KV_RANK, HEAD_DIM), jnp.bfloat16),
            ((224, 1024), jnp.bfloat16),
            ((8, 128), jnp.float32),
        ],
        [SMEM] + [HBM] * 3 + [VMEM] * 3,
        [
            pltpu.VMEM((8, HEAD_DIM, KV_RANK), jnp.bfloat16),
            pltpu.VMEM((128, 1024), jnp.bfloat16),
            pltpu.VMEM((128, 512), jnp.bfloat16),
            pltpu.SemaphoreType.DMA((3,)),
        ],
        limit=16,
        flops=700_000_000,
        name="queries",
    )(place, q_nope, q_rope, w_out.T, docs, ups, moved(ups, other_core))

    low, high = call(
        gate_kernel,
        [((2, 128, WIDE), jnp.bfloat16)] * 2,
        [VMEM] * 3,
        limit=8,
        name="gate",
    )(*pieces[1:], token)
    weights = [weight] + [moved(weight, flip_z(bits)) for bits in (1, 2, 3)]
    pieces = [twelve, low, high, theirs, moved(low, other_core), moved(high, other_core)]
    values, log_sum = call(
        attention_kernel,
        [((1024, 128), jnp.bfloat16), ((8, 128), jnp.float32)],
        [SMEM] + [VMEM] * 8,
        [
            pltpu.VMEM((4096, WIDE), jnp.bfloat16),
            pltpu.VMEM((4096 // TILE, 1024, TILE), jnp.float32),
            pltpu.VMEM((1024, 128), jnp.float32),
            pltpu.VMEM((1024, 128), jnp.float32),
            pltpu.VMEM((1024, KV_RANK), jnp.float32),
        ],
        limit=32,
        flops=10_000_000_000,
        name="attention",
    )(place, query, up_value, *pieces)

    (values,) = call(
        hold_kernel, [((1024, 128), jnp.bfloat16)], [VMEM] * 2, limit=8, name="hold"
    )(values, weights[1])
    right, left = moved(values, along_x(-1)), moved(values, along_x(1))
    low, high = call(
        outer_kernel, [((512, 128), jnp.bfloat16)] * 2, [VMEM] * 2, limit=8, name="outer"
    )(right, left)
    low, high = moved(low, along_x(-1)), moved(high, along_x(1))
    (gathered,) = call(
        third_kernel, [((4, 1024, 128), jnp.bfloat16)], [SMEM] + [VMEM] * 7, limit=8, name="third"
    )(x.reshape(1).astype(jnp.int32), values, right, left, low, high, *weights[2:])
    order = jnp.stack([z, (y + 2) % 4, (y + 1) % 4, (y + 3) % 4, y, half]).astype(jnp.int32)
    theirs = moved(gathered, other_core)
    term, pair = ((2, 224, 256), jnp.bfloat16), [((224, 256), jnp.bfloat16)] * 2
    far_give, left_give, held = call(
        first_terms_kernel,
        [term] * 2 + [((2, 2, 224, 1024), jnp.bfloat16)],
        [SMEM] + [VMEM] * 2 + [ANY] * 4,
        [pltpu.SemaphoreType.DMA((4,))],
        limit=16,
        flops=470_000_000,
        name="project",
    )(order, gathered, theirs, *weights)
    (terms,) = call(
        other_terms_kernel,
        [((6, 2, 224, 256), jnp.bfloat16)],
        [SMEM] + [VMEM] * 3,
        limit=16,
        flops=1_410_000_000,
        name="others",
    )(order, gathered, theirs, held)
    low = jnp.stack([x % 2, core]).astype(jnp.int32)
    left_give = moved(left_give, along_y(-1))
    right_give, far_keep = call(
        early_kernel, [term] * 2, [VMEM] * 3, limit=16, name="early"
    )(terms, moved(far_give, along_y(1)), left_give)
    same, cross, left_keep, right_keep = call(
        give_kernel,
        pair + [term] * 2,
        [SMEM] + [VMEM] * 4,
        [pltpu.VMEM((2, 224, 256), jnp.bfloat16)],
        limit=16,
        name="give",
    )(low, terms, moved(right_give, along_y(1)), left_give, moved(far_keep, along_y(-1)))
    give = [moved(same, settle(False, True)), moved(cross, settle(True, True))]
    same, cross = call(
        keep_kernel,
        pair,
        [SMEM] + [VMEM] * 3,
        [pltpu.VMEM((2, 224, 256), jnp.bfloat16)],
        limit=16,
        name="keep",
    )(low, terms, moved(right_keep, along_y(1)), moved(left_keep, along_y(-1)))
    keep = [moved(same, settle(False, False)), moved(cross, settle(True, False))]
    mine, theirs = call(
        halves_kernel, [((2, 224, 128), jnp.bfloat16)] * 2, [VMEM] * 4, limit=16, name="halves"
    )(*give, *keep)
    (mixed,) = call(
        finish_kernel,
        [((128, 896), jnp.bfloat16)],
        [SMEM] + [VMEM] * 2,
        [pltpu.VMEM((4, 224, 128), jnp.float32)],
        limit=16,
        name="finish",
    )(low, mine, moved(theirs, other_core))
    return (mixed, log_sum.T)


def solution(mesh):
    return jax.shard_map(
        per_device,
        mesh=mesh,
        in_specs=(
            P("ctx", "dp"),
            P("ctx", "dp"),
            P("ctx", None),
            P("ctx", None),
            P("ctx"),
            P("dp", "ctx", None),
            P("dp", "ctx", None),
            P("dp", "ctx"),
        ),
        out_specs=(P("ctx", "dp"), P("ctx", "dp")),
        check_vma=False,
    )
```

```python
import jax
import jax.numpy as jnp
from jax import lax
from jax.experimental import pallas as pl
from jax.experimental.pallas import tpu as pltpu
from jax.sharding import PartitionSpec as P

HEAD_DIM = 128
KV_RANK = 512
ROPE_DIM = 64
WIDE = 640
TILE = 512
CHUNK = 256
FAR = -1e30
LOG2E = 1.4426950408889634
SCALE = (HEAD_DIM + ROPE_DIM) ** (-0.5)
AXES = ("ctx", "dp")
MIB = 1024 * 1024
VMEM = pl.BlockSpec(memory_space=pltpu.VMEM)
SMEM = pl.BlockSpec(memory_space=pltpu.SMEM)
ANY = pl.BlockSpec(memory_space=pl.ANY)
HBM = pl.BlockSpec(memory_space=pltpu.HBM)


def moved(array, to):
    pairs = []
    for ctx in range(32):
        for dp in range(8):
            z, x, core, half, y = to(ctx // 8, ctx // 2 % 4, ctx % 2, dp // 4, dp % 4)
            pairs.append((ctx * 8 + dp, (z * 8 + x * 2 + core) * 8 + half * 4 + y))
    return lax.ppermute(array, AXES, pairs)


def along_x(by):
    return lambda z, x, core, half, y: (z, (x + by) % 4, core, half, y)


def along_y(by):
    return lambda z, x, core, half, y: (z, x, core, half, (y + by) % 4)


def along_z_ring(by):
    def to(z, x, core, half, y):
        whole = (half * 4 + z + by) % 8
        return (whole % 4, x, core, whole // 4, y)

    return to


def flip_z(bit):
    return lambda z, x, core, half, y: (z ^ bit, x, core, half, y)


def other_core(z, x, core, half, y):
    return (z, x, 1 - core, half, y)


def settle(cross, over):
    def to(z, x, core, half, y):
        low = 1 - x % 2 if cross else x % 2
        return (z, y % 2 * 2 + low, core, 1 - half if over else half, y // 2 * 2 + x // 2)

    return to


def contract_last(left, right):
    return lax.dot_general(left, right, (((1,), (1,)), ((), ())), preferred_element_type=jnp.float32)


def call(kernel, outs, in_specs, scratch=(), limit=32, flops=0, name=None):
    return pl.pallas_call(
        kernel,
        out_shape=tuple(jax.ShapeDtypeStruct(*out) for out in outs),
        in_specs=in_specs,
        out_specs=tuple(VMEM for _ in outs),
        scratch_shapes=list(scratch),
        compiler_params=pltpu.CompilerParams(vmem_limit_bytes=limit * MIB),
        cost_estimate=pl.CostEstimate(flops=flops, bytes_accessed=3 * MIB, transcendentals=0),
        name=name,
    )


def doc_columns(docs):
    return jnp.transpose(jnp.broadcast_to(docs.astype(jnp.float32), (128, 128)))


def fetched(pairs, sems):
    copies = [pltpu.make_async_copy(a, b, sems.at[n]) for n, (a, b) in enumerate(pairs)]
    for copy in copies:
        copy.start()
    return copies


def keys_kernel(latent_in, rope_in, docs_in, out, rope_key, docs, sems):
    copies = fetched(
        [(latent_in, out.at[:, 0:KV_RANK]), (rope_in, rope_key), (docs_in, docs)], sems
    )
    for copy in copies:
        copy.wait()
    rope = jnp.transpose(rope_key[...].astype(jnp.float32))
    doc = doc_columns(docs[...])
    lane = lax.broadcasted_iota(jnp.int32, (128, 128), 1)
    place = (lane - ROPE_DIM).astype(jnp.float32)
    tail = jnp.where(place == doc, 1.0, jnp.where(lane == ROPE_DIM + 4, doc, 0.0))
    tail = jnp.where(lane < ROPE_DIM, jnp.concatenate([rope, rope], axis=1), tail)
    out[:, KV_RANK:WIDE] = tail.astype(jnp.bfloat16)


def first_kernel(*refs):
    row, line = refs[-2:]
    for n in range(4):
        row[n] = refs[n][...]
        line[n] = refs[4 + n][...]


def second_kernel(row, plus, minus, *rest):
    ring, (low, high, twelve, ups) = rest[:4], rest[4:]
    low[...] = plus[0:2]
    high[...] = minus[2:4]
    for n, part in enumerate((row, plus, minus)):
        twelve[4 * n : 4 * n + 4] = part[...]
    for n in range(4):
        ups[n] = ring[n][...]


def outer_kernel(right, left, low, high):
    low[...] = right[0:512]
    high[...] = left[512:1024]


def gate_kernel(low_in, high_in, token, low, high):
    low[...] = low_in[...]
    high[...] = high_in[...]


def hold_kernel(values_in, weight, values):
    values[...] = values_in[...]


def queries_kernel(place, q_nope_in, q_rope_in, weight_in, docs, mine, theirs, *rest):
    query, up_value, weight, token, up_key, q_nope, q_rope, sems = rest
    token[...] = jnp.zeros((8, 128), jnp.float32)
    copies = fetched([(q_nope_in, q_nope), (q_rope_in, q_rope), (weight_in, weight)], sems)
    z, x, core = place[0], place[1], place[2]
    row = lax.broadcasted_iota(jnp.int32, (512, 1), 0)
    position = row % 128 // 4
    slot = ((position % 2) ^ core) * 16 + ((position // 2 % 4 - x) & 3) * 4 + ((position // 8) ^ z)
    wanted = slot * 16 + row // 128 * 4 + row % 4
    pick = (lax.broadcasted_iota(jnp.int32, (512, 512), 1) == wanted).astype(jnp.float32)
    pick = pick.astype(jnp.bfloat16)
    for h in range(0, 8, 2):
        both = [
            jnp.concatenate(
                [side[:, :, n].reshape(256, 128) for side in (mine, theirs)], axis=0
            )
            for n in (h, h + 1)
        ]
        ordered = jnp.dot(pick, jnp.concatenate(both, axis=1), preferred_element_type=jnp.float32)
        ordered = ordered.astype(jnp.bfloat16)
        for n in (0, 1):
            for j in range(4):
                up_key[h + n, :, j * 128 : j * 128 + 128] = ordered[
                    j * 128 : j * 128 + 128, n * 128 : n * 128 + 128
                ]
    for side, array in enumerate((mine, theirs)):
        for dx in range(4):
            for dz in range(4):
                at = (z ^ dz) * 8 + ((x + dx) & 3) * 2 + (core ^ side)
                up_value[:, pl.ds(pl.multiple_of(at * 16, 16), 16), :] = array[dx, dz, 8:16]
    doc = doc_columns(docs[...])
    lane = lax.broadcasted_iota(jnp.int32, (128, 128), 1)
    other_doc = (lane >= ROPE_DIM) & (lane < ROPE_DIM + 4)
    other_doc = other_doc & ((lane - ROPE_DIM).astype(jnp.float32) != doc)
    marks = jnp.where(other_doc, FAR, 0.0).astype(jnp.bfloat16)[:, ROPE_DIM:]
    for copy in copies:
        copy.wait()
    for h in range(8):
        rows = pl.ds(h * 128, 128)
        latent_part = jnp.dot(
            q_nope[:, h * 128 : h * 128 + 128], up_key[h], preferred_element_type=jnp.float32
        )
        query[rows, 0:KV_RANK] = latent_part.astype(jnp.bfloat16)
        query[rows, KV_RANK:WIDE] = jnp.concatenate(
            [q_rope[:, h * 64 : h * 64 + 64], marks], axis=1
        )


def attention_kernel(place, query, up_value, *rest):
    pieces, (values, log_sum, keys, score, total, peak, weighed) = rest[:6], rest[6:]
    z, x, core = place[0], place[1], place[2]
    blocks = TILE // 128
    own_tile = lax.div(place[3], blocks)

    for side in range(2):
        twelve, two_low, two_high = pieces[side * 3 : side * 3 + 3]
        for dz, dx in [(a, b) for a in range(4) for b in range(4)]:
            block = (((z + dz) & 3) * 4 + ((x + dx) & 3)) * 2 + (core ^ side)

            @pl.when(block < (own_tile + 1) * blocks)
            def _():
                rows = pl.ds(pl.multiple_of(block * 128, 128), 128)
                if dz == 2:
                    keys[rows, :] = two_low[dx] if dx < 2 else two_high[dx - 2]
                else:
                    keys[rows, :] = twelve[{0: 0, 1: 4, 3: 8}[dz] + dx]

    def lane_groups(array, join):
        parts = [array[:, n * 128 : n * 128 + 128] for n in range(TILE // 128)]
        return join(join(parts[0], parts[1]), join(parts[2], parts[3]))

    def scores(tile, first):
        start = pl.multiple_of(tile * TILE, TILE)
        for part in range(1024 // CHUNK):
            rows = pl.ds(part * CHUNK, CHUNK)
            new = contract_last(query[rows, :], keys[pl.ds(start, TILE), :])
            if first:
                at = lax.broadcasted_iota(jnp.int32, (CHUNK, TILE), 0)
                row_place = place[3] * 128 + (at & 127)
                key_place = start + lax.broadcasted_iota(jnp.int32, (CHUNK, TILE), 1)
                new = jnp.where(key_place <= row_place, new, FAR)
            score[tile, rows, :] = new
            best = lane_groups(new, jnp.maximum)
            peak[rows, :] = best if first else jnp.maximum(peak[rows, :], best)

    def weigh(tile, first):
        start = pl.multiple_of(tile * TILE, TILE)
        for part in range(1024 // CHUNK):
            rows = pl.ds(part * CHUNK, CHUNK)
            top = peak[rows, :]
            top = jnp.concatenate([top] * (TILE // 128), axis=1)
            expon = jnp.exp2((score[tile, rows, :] - top) * (SCALE * LOG2E))
            lanes = lane_groups(expon, jnp.add)
            product = jnp.dot(
                expon.astype(jnp.bfloat16),
                keys[pl.ds(start, TILE), 0:KV_RANK],
                preferred_element_type=jnp.float32,
            )
            total[rows, :] = lanes if first else total[rows, :] + lanes
            weighed[rows, :] = product if first else weighed[rows, :] + product

    def each_before(do):
        lax.fori_loop(low, own_tile, lambda tile, carry: (do(tile, False), carry)[1], 0)

    scores(own_tile, True)
    lane = lax.broadcasted_iota(jnp.int32, (16, 128), 1)
    row_at = lax.broadcasted_iota(jnp.int32, (16, 128), 0)
    earlier = jnp.zeros((16, 128), jnp.float32)
    for tile in range(4096 // TILE):
        last = keys[tile * TILE + TILE - 16 : tile * TILE + TILE, KV_RANK:WIDE].astype(jnp.float32)
        before = (last < place[4].astype(jnp.float32)) & (jnp.int32(tile) < own_tile)
        earlier = earlier + jnp.where(before, 1.0, 0.0)
    here = (lane == ROPE_DIM + 4) & (row_at == 15)
    low = jnp.max(jnp.where(here, earlier, 0.0)).astype(jnp.int32)
    each_before(scores)
    for part in range(1024 // CHUNK):
        rows = pl.ds(part * CHUNK, CHUNK)
        top = jnp.max(peak[rows, :], axis=1, keepdims=True)
        peak[rows, :] = jnp.broadcast_to(top, (CHUNK, 128))
    weigh(own_tile, True)
    each_before(weigh)

    column = lax.broadcasted_iota(jnp.int32, (128, 128), 1)
    logs = jnp.zeros((128, 128), jnp.float32)
    for h in range(8):
        rows = pl.ds(h * 128, 128)
        whole = jnp.sum(total[rows, :], axis=1, keepdims=True)
        attended = (weighed[rows, :] * (1.0 / whole)).astype(jnp.bfloat16)
        value = jnp.dot(attended, up_value[h], preferred_element_type=jnp.float32)
        values[h * 128 : h * 128 + 128, :] = jnp.transpose(value).astype(jnp.bfloat16)
        logs = jnp.where(column == h, peak[rows, :] * SCALE + jnp.log(whole), logs)
    log_sum[...] = jnp.transpose(logs)[0:8, :]


def third_kernel(place, own, right, left, low, high, *rest):
    out = rest[-1]
    for dx, array in ((0, own), (1, right), (3, left)):
        out[(place[0] + dx) & 3] = array[...]
    out[(place[0] + 2) & 3, 0:512] = low[...]
    out[(place[0] + 2) & 3, 512:1024] = high[...]


def project_kernel(wanted, place, mine, theirs, weights, outs):
    for chip in sorted({chip for chip, _ in wanted}):
        high, low = lax.div(place[1 + chip], 2), place[1 + chip] & 1
        right = jnp.concatenate(
            [mine[2 * low], theirs[2 * low], mine[2 * low + 1], theirs[2 * low + 1]], axis=1
        )
        halves = [half for other, half in wanted if other == chip]
        weight = weights[high, halves[0] : halves[-1] + 1].reshape(224 * len(halves), 1024)
        terms = jnp.dot(weight, right, preferred_element_type=jnp.float32).astype(jnp.bfloat16)
        for n, half in enumerate(halves):
            out = outs[wanted.index((chip, half))]
            for low_bit in range(2):
                out[low_bit] = terms[
                    n * 224 : n * 224 + 224, low_bit * 256 : low_bit * 256 + 256
                ]


def first_terms_kernel(place, mine, theirs, *rest):
    blocks, (far_give, left_give, weights, sems) = rest[:4], rest[4:]
    copies = []
    for dz in range(4):
        at = place[0] ^ dz
        copies.append((blocks[dz], weights.at[at & 1, 1 - (lax.div(at, 2) ^ place[5])]))
    copies = fetched(copies, sems)
    for copy in copies:
        copy.wait()
    project_kernel([(0, 0), (2, 0)], place, mine, theirs, weights, [far_give, left_give])


def other_terms_kernel(place, mine, theirs, weights, out):
    wanted = [(0, 1), (1, 0), (1, 1), (2, 1), (3, 0), (3, 1)]
    project_kernel(wanted, place, mine, theirs, weights, [out.at[n] for n in range(6)])


def summed(*arrays):
    whole = arrays[0][...].astype(jnp.float32)
    for array in arrays[1:]:
        whole = whole + array[...].astype(jnp.float32)
    return whole.astype(jnp.bfloat16)


def early_kernel(terms, far_give, left_give, out, far_out, part):
    part[...] = terms[4].astype(jnp.float32) + left_give[...].astype(jnp.float32)
    out[...] = summed(terms.at[1], far_give)
    far_out[...] = terms[0]


def give_kernel(place, terms, left, right, far_keep, *outs):
    same, cross, left_out, right_out, whole = outs
    whole[...] = summed(left, right)
    same[...] = whole[place[0]]
    cross[...] = whole[1 - place[0]]
    left_out[...] = summed(terms.at[3], far_keep)
    right_out[...] = terms[2]


def keep_kernel(place, terms, left, right, same, cross, whole):
    whole[...] = summed(terms.at[5], left, right)
    same[...] = whole[place[0]]
    cross[...] = whole[1 - place[0]]


def halves_kernel(give_same, give_cross, keep_same, keep_cross, mine, theirs):
    for cross, pair in enumerate(((keep_same, give_same), (keep_cross, give_cross))):
        whole = summed(*pair)
        mine[cross] = whole[:, 0:128]
        theirs[cross] = whole[:, 128:256]


def finish_kernel(place, mine, theirs, mixed, whole):
    for cross in range(2):
        for side, array in enumerate((mine, theirs)):
            whole[(place[0] ^ cross) * 2 + (place[1] ^ side)] = array[cross].astype(jnp.float32)
    mixed[...] = jnp.transpose(whole[...].reshape(896, 128)).astype(jnp.bfloat16)


def gather_ring(block):
    return [block] + [moved(block, along_x(-by)) for by in (1, 2, 3)]


def per_device(q_nope, q_rope, latent, rope_key, segment_ids, w_uk, w_uv, w_out):
    ctx, dp = lax.axis_index("ctx"), lax.axis_index("dp")
    z, x, core = ctx // 8, ctx // 2 % 4, ctx % 2
    half, y = dp // 4, dp % 4
    place = jnp.stack([z, x, core, ctx, segment_ids[0]]).astype(jnp.int32)
    docs = segment_ids.reshape(1, 128)

    (block,) = call(
        keys_kernel,
        [((128, WIDE), jnp.bfloat16)],
        [HBM] * 3,
        [
            pltpu.VMEM((ROPE_DIM, 128), jnp.bfloat16),
            pltpu.VMEM((1, 128), jnp.int32),
            pltpu.SemaphoreType.DMA((3,)),
        ],
        limit=8,
        name="keys",
    )(latent, rope_key.T, docs)
    up = w_uk.reshape(8, 4, 4, 128).transpose(0, 2, 1, 3).reshape(8, 16, 128)
    up = jnp.concatenate([up, w_uv])
    ring = gather_ring(block)
    line = [up] + [moved(up, flip_z(bits)) for bits in (1, 2, 3)]
    row, line = call(
        first_kernel,
        [((4, 128, WIDE), jnp.bfloat16), ((4, 16, 16, 128), jnp.bfloat16)],
        [VMEM] * 8,
        limit=16,
        name="first",
    )(*ring, *line)
    plus, minus = moved(row, along_z_ring(-1)), moved(row, along_z_ring(1))
    low, high, twelve, ups = call(
        second_kernel,
        [
            ((2, 128, WIDE), jnp.bfloat16),
            ((2, 128, WIDE), jnp.bfloat16),
            ((12, 128, WIDE), jnp.bfloat16),
            ((4, 4, 16, 16, 128), jnp.bfloat16),
        ],
        [VMEM] * 7,
        limit=16,
        name="second",
    )(row, plus, minus, *gather_ring(line))
    pieces = [twelve, moved(low, along_z_ring(-1)), moved(high, along_z_ring(1))]
    theirs = moved(twelve, other_core)

    query, up_value, weight, token = call(
        queries_kernel,
        [
            ((1024, WIDE), jnp.bfloat16),
            ((8, KV_RANK, HEAD_DIM), jnp.bfloat16),
            ((224, 1024), jnp.bfloat16),
            ((8, 128), jnp.float32),
        ],
        [SMEM] + [HBM] * 3 + [VMEM] * 3,
        [
            pltpu.VMEM((8, HEAD_DIM, KV_RANK), jnp.bfloat16),
            pltpu.VMEM((128, 1024), jnp.bfloat16),
            pltpu.VMEM((128, 512), jnp.bfloat16),
            pltpu.SemaphoreType.DMA((3,)),
        ],
        limit=16,
        flops=700_000_000,
        name="queries",
    )(place, q_nope, q_rope, w_out.T, docs, ups, moved(ups, other_core))

    low, high = call(
        gate_kernel,
        [((2, 128, WIDE), jnp.bfloat16)] * 2,
        [VMEM] * 3,
        limit=8,
        name="gate",
    )(*pieces[1:], token)
    weights = [weight] + [moved(weight, flip_z(bits)) for bits in (1, 2, 3)]
    pieces = [twelve, low, high, theirs, moved(low, other_core), moved(high, other_core)]
    values, log_sum = call(
        attention_kernel,
        [((1024, 128), jnp.bfloat16), ((8, 128), jnp.float32)],
        [SMEM] + [VMEM] * 8,
        [
            pltpu.VMEM((4096, WIDE), jnp.bfloat16),
            pltpu.VMEM((4096 // TILE, 1024, TILE), jnp.float32),
            pltpu.VMEM((1024, 128), jnp.float32),
            pltpu.VMEM((1024, 128), jnp.float32),
            pltpu.VMEM((1024, KV_RANK), jnp.float32),
        ],
        limit=32,
        flops=10_000_000_000,
        name="attention",
    )(place, query, up_value, *pieces)

    (values,) = call(
        hold_kernel, [((1024, 128), jnp.bfloat16)], [VMEM] * 2, limit=8, name="hold"
    )(values, weights[1])
    right, left = moved(values, along_x(-1)), moved(values, along_x(1))
    low, high = call(
        outer_kernel, [((512, 128), jnp.bfloat16)] * 2, [VMEM] * 2, limit=8, name="outer"
    )(right, left)
    low, high = moved(low, along_x(-1)), moved(high, along_x(1))
    (gathered,) = call(
        third_kernel, [((4, 1024, 128), jnp.bfloat16)], [SMEM] + [VMEM] * 7, limit=8, name="third"
    )(x.reshape(1).astype(jnp.int32), values, right, left, low, high, *weights[2:])
    order = jnp.stack([z, (y + 2) % 4, (y + 1) % 4, (y + 3) % 4, y, half]).astype(jnp.int32)
    theirs = moved(gathered, other_core)
    term, pair = ((2, 224, 256), jnp.bfloat16), [((224, 256), jnp.bfloat16)] * 2
    far_give, left_give, held = call(
        first_terms_kernel,
        [term] * 2 + [((2, 2, 224, 1024), jnp.bfloat16)],
        [SMEM] + [VMEM] * 2 + [ANY] * 4,
        [pltpu.SemaphoreType.DMA((4,))],
        limit=16,
        flops=470_000_000,
        name="project",
    )(order, gathered, theirs, *weights)
    (terms,) = call(
        other_terms_kernel,
        [((6, 2, 224, 256), jnp.bfloat16)],
        [SMEM] + [VMEM] * 3,
        limit=16,
        flops=1_410_000_000,
        name="others",
    )(order, gathered, theirs, held)
    low = jnp.stack([x % 2, core]).astype(jnp.int32)
    left_give = moved(left_give, along_y(-1))
    right_give, far_keep, left_give = call(
        early_kernel, [term] * 2 + [((2, 224, 256), jnp.float32)], [VMEM] * 3, limit=16, name="early"
    )(terms, moved(far_give, along_y(1)), left_give)
    same, cross, left_keep, right_keep = call(
        give_kernel,
        pair + [term] * 2,
        [SMEM] + [VMEM] * 4,
        [pltpu.VMEM((2, 224, 256), jnp.bfloat16)],
        limit=16,
        name="give",
    )(low, terms, moved(right_give, along_y(1)), left_give, moved(far_keep, along_y(-1)))
    give = [moved(same, settle(False, True)), moved(cross, settle(True, True))]
    same, cross = call(
        keep_kernel,
        pair,
        [SMEM] + [VMEM] * 3,
        [pltpu.VMEM((2, 224, 256), jnp.bfloat16)],
        limit=16,
        name="keep",
    )(low, terms, moved(right_keep, along_y(1)), moved(left_keep, along_y(-1)))
    keep = [moved(same, settle(False, False)), moved(cross, settle(True, False))]
    mine, theirs = call(
        halves_kernel, [((2, 224, 128), jnp.bfloat16)] * 2, [VMEM] * 4, limit=16, name="halves"
    )(*give, *keep)
    (mixed,) = call(
        finish_kernel,
        [((128, 896), jnp.bfloat16)],
        [SMEM] + [VMEM] * 2,
        [pltpu.VMEM((4, 224, 128), jnp.float32)],
        limit=16,
        name="finish",
    )(low, mine, moved(theirs, other_core))
    return (mixed, log_sum.T)


def solution(mesh):
    return jax.shard_map(
        per_device,
        mesh=mesh,
        in_specs=(
            P("ctx", "dp"),
            P("ctx", "dp"),
            P("ctx", None),
            P("ctx", None),
            P("ctx"),
            P("dp", "ctx", None),
            P("dp", "ctx", None),
            P("dp", "ctx"),
        ),
        out_specs=(P("ctx", "dp"), P("ctx", "dp")),
        check_vma=False,
    )
```

```python
import jax
import jax.numpy as jnp
from jax import lax
from jax.experimental import pallas as pl
from jax.experimental.pallas import tpu as pltpu
from jax.sharding import PartitionSpec as P

HEAD_DIM = 128
KV_RANK = 512
ROPE_DIM = 64
WIDE = 640
TILE = 512
CHUNK = 256
FAR = -1e30
LOG2E = 1.4426950408889634
SCALE = (HEAD_DIM + ROPE_DIM) ** (-0.5)
AXES = ("ctx", "dp")
MIB = 1024 * 1024
VMEM = pl.BlockSpec(memory_space=pltpu.VMEM)
SMEM = pl.BlockSpec(memory_space=pltpu.SMEM)
ANY = pl.BlockSpec(memory_space=pl.ANY)
HBM = pl.BlockSpec(memory_space=pltpu.HBM)


def moved(array, to):
    pairs = []
    for ctx in range(32):
        for dp in range(8):
            z, x, core, half, y = to(ctx // 8, ctx // 2 % 4, ctx % 2, dp // 4, dp % 4)
            pairs.append((ctx * 8 + dp, (z * 8 + x * 2 + core) * 8 + half * 4 + y))
    return lax.ppermute(array, AXES, pairs)


def along_x(by):
    return lambda z, x, core, half, y: (z, (x + by) % 4, core, half, y)


def along_y(by):
    return lambda z, x, core, half, y: (z, x, core, half, (y + by) % 4)


def along_z_ring(by):
    def to(z, x, core, half, y):
        whole = (half * 4 + z + by) % 8
        return (whole % 4, x, core, whole // 4, y)

    return to


def flip_z(bit):
    return lambda z, x, core, half, y: (z ^ bit, x, core, half, y)


def other_core(z, x, core, half, y):
    return (z, x, 1 - core, half, y)


def settle(cross, over):
    def to(z, x, core, half, y):
        low = 1 - x % 2 if cross else x % 2
        return (z, y % 2 * 2 + low, core, 1 - half if over else half, y // 2 * 2 + x // 2)

    return to


def contract_last(left, right):
    return lax.dot_general(left, right, (((1,), (1,)), ((), ())), preferred_element_type=jnp.float32)


def call(kernel, outs, in_specs, scratch=(), limit=32, flops=0, name=None):
    return pl.pallas_call(
        kernel,
        out_shape=tuple(jax.ShapeDtypeStruct(*out) for out in outs),
        in_specs=in_specs,
        out_specs=tuple(VMEM for _ in outs),
        scratch_shapes=list(scratch),
        compiler_params=pltpu.CompilerParams(vmem_limit_bytes=limit * MIB),
        cost_estimate=pl.CostEstimate(flops=flops, bytes_accessed=3 * MIB, transcendentals=0),
        name=name,
    )


def doc_columns(docs):
    return jnp.transpose(jnp.broadcast_to(docs.astype(jnp.float32), (128, 128)))


def fetched(pairs, sems):
    copies = [pltpu.make_async_copy(a, b, sems.at[n]) for n, (a, b) in enumerate(pairs)]
    for copy in copies:
        copy.start()
    return copies


def keys_kernel(latent_in, tail_in, out, sems):
    copies = fetched([(latent_in, out.at[:, 0:KV_RANK])], sems)
    tail = jnp.transpose(tail_in[...].astype(jnp.float32))
    lane = lax.broadcasted_iota(jnp.int32, (128, 128), 1)
    same = (lane - ROPE_DIM).astype(jnp.float32) == tail
    marks = jnp.where(same, 1.0, jnp.where(lane == ROPE_DIM + 4, tail, 0.0))
    out[:, KV_RANK:WIDE] = jnp.where(lane < ROPE_DIM, tail, marks).astype(jnp.bfloat16)
    for copy in copies:
        copy.wait()


def first_kernel(*refs):
    row, line = refs[-2:]
    for n in range(4):
        row[n] = refs[n][...]
        line[n] = refs[4 + n][...]


def second_kernel(row, plus, minus, *rest):
    ring, (low, high, twelve, ups) = rest[:4], rest[4:]
    low[...] = plus[0:2]
    high[...] = minus[2:4]
    for n, part in enumerate((row, plus, minus)):
        twelve[4 * n : 4 * n + 4] = part[...]
    for n in range(4):
        ups[n] = ring[n][...]


def outer_kernel(right, left, low, high):
    low[...] = right[0:512]
    high[...] = left[512:1024]


def gate_kernel(low_in, high_in, token, low, high):
    low[...] = low_in[...]
    high[...] = high_in[...]


def hold_kernel(values_in, weight, values):
    values[...] = values_in[...]


def queries_kernel(place, q_nope_in, q_rope_in, weight_in, docs, mine, theirs, *rest):
    query, up_value, weight, token, up_key, q_nope, q_rope, sems = rest
    token[...] = jnp.zeros((8, 128), jnp.float32)
    copies = fetched([(q_nope_in, q_nope), (q_rope_in, q_rope), (weight_in, weight)], sems)
    z, x, core = place[0], place[1], place[2]
    row = lax.broadcasted_iota(jnp.int32, (512, 1), 0)
    position = row % 128 // 4
    slot = ((position % 2) ^ core) * 16 + ((position // 2 % 4 - x) & 3) * 4 + ((position // 8) ^ z)
    wanted = slot * 16 + row // 128 * 4 + row % 4
    pick = (lax.broadcasted_iota(jnp.int32, (512, 512), 1) == wanted).astype(jnp.float32)
    pick = pick.astype(jnp.bfloat16)
    for h in range(0, 8, 2):
        both = [
            jnp.concatenate(
                [side[:, :, n].reshape(256, 128) for side in (mine, theirs)], axis=0
            )
            for n in (h, h + 1)
        ]
        ordered = jnp.dot(pick, jnp.concatenate(both, axis=1), preferred_element_type=jnp.float32)
        ordered = ordered.astype(jnp.bfloat16)
        for n in (0, 1):
            for j in range(4):
                up_key[h + n, :, j * 128 : j * 128 + 128] = ordered[
                    j * 128 : j * 128 + 128, n * 128 : n * 128 + 128
                ]
    for side, array in enumerate((mine, theirs)):
        for dx in range(4):
            for dz in range(4):
                at = (z ^ dz) * 8 + ((x + dx) & 3) * 2 + (core ^ side)
                up_value[:, pl.ds(pl.multiple_of(at * 16, 16), 16), :] = array[dx, dz, 8:16]
    doc = doc_columns(docs[...])
    lane = lax.broadcasted_iota(jnp.int32, (128, 128), 1)
    other_doc = (lane >= ROPE_DIM) & (lane < ROPE_DIM + 4)
    other_doc = other_doc & ((lane - ROPE_DIM).astype(jnp.float32) != doc)
    marks = jnp.where(other_doc, FAR, 0.0).astype(jnp.bfloat16)[:, ROPE_DIM:]
    for copy in copies:
        copy.wait()
    for h in range(8):
        rows = pl.ds(h * 128, 128)
        latent_part = jnp.dot(
            q_nope[:, h * 128 : h * 128 + 128], up_key[h], preferred_element_type=jnp.float32
        )
        query[rows, 0:KV_RANK] = latent_part.astype(jnp.bfloat16)
        query[rows, KV_RANK:WIDE] = jnp.concatenate(
            [q_rope[:, h * 64 : h * 64 + 64], marks], axis=1
        )


def attention_kernel(place, query, up_value, *rest):
    pieces, (values, log_sum, keys, score, total, peak, weighed) = rest[:6], rest[6:]
    z, x, core = place[0], place[1], place[2]
    blocks = TILE // 128
    own_tile = lax.div(place[3], blocks)

    for side in range(2):
        twelve, two_low, two_high = pieces[side * 3 : side * 3 + 3]
        for dz, dx in [(a, b) for a in range(4) for b in range(4)]:
            block = (((z + dz) & 3) * 4 + ((x + dx) & 3)) * 2 + (core ^ side)

            @pl.when(block < (own_tile + 1) * blocks)
            def _():
                rows = pl.ds(pl.multiple_of(block * 128, 128), 128)
                if dz == 2:
                    keys[rows, :] = two_low[dx] if dx < 2 else two_high[dx - 2]
                else:
                    keys[rows, :] = twelve[{0: 0, 1: 4, 3: 8}[dz] + dx]

    def lane_groups(array, join):
        parts = [array[:, n * 128 : n * 128 + 128] for n in range(TILE // 128)]
        return join(join(parts[0], parts[1]), join(parts[2], parts[3]))

    def scores(tile, first):
        start = pl.multiple_of(tile * TILE, TILE)
        for part in range(1024 // CHUNK):
            rows = pl.ds(part * CHUNK, CHUNK)
            new = contract_last(query[rows, :], keys[pl.ds(start, TILE), :])
            if first:
                at = lax.broadcasted_iota(jnp.int32, (CHUNK, TILE), 0)
                row_place = place[3] * 128 + (at & 127)
                key_place = start + lax.broadcasted_iota(jnp.int32, (CHUNK, TILE), 1)
                new = jnp.where(key_place <= row_place, new, FAR)
            score[tile, rows, :] = new
            best = lane_groups(new, jnp.maximum)
            peak[rows, :] = best if first else jnp.maximum(peak[rows, :], best)

    def weigh(tile, first):
        start = pl.multiple_of(tile * TILE, TILE)
        for part in range(1024 // CHUNK):
            rows = pl.ds(part * CHUNK, CHUNK)
            top = peak[rows, :]
            top = jnp.concatenate([top] * (TILE // 128), axis=1)
            expon = jnp.exp2((score[tile, rows, :] - top) * (SCALE * LOG2E))
            lanes = lane_groups(expon, jnp.add)
            product = jnp.dot(
                expon.astype(jnp.bfloat16),
                keys[pl.ds(start, TILE), 0:KV_RANK],
                preferred_element_type=jnp.float32,
            )
            total[rows, :] = lanes if first else total[rows, :] + lanes
            weighed[rows, :] = product if first else weighed[rows, :] + product

    def each_before(do):
        lax.fori_loop(low, own_tile, lambda tile, carry: (do(tile, False), carry)[1], 0)

    scores(own_tile, True)
    lane = lax.broadcasted_iota(jnp.int32, (16, 128), 1)
    row_at = lax.broadcasted_iota(jnp.int32, (16, 128), 0)
    earlier = jnp.zeros((16, 128), jnp.float32)
    for tile in range(4096 // TILE):
        last = keys[tile * TILE + TILE - 16 : tile * TILE + TILE, KV_RANK:WIDE].astype(jnp.float32)
        before = (last < place[4].astype(jnp.float32)) & (jnp.int32(tile) < own_tile)
        earlier = earlier + jnp.where(before, 1.0, 0.0)
    here = (lane == ROPE_DIM + 4) & (row_at == 15)
    low = jnp.max(jnp.where(here, earlier, 0.0)).astype(jnp.int32)
    each_before(scores)
    for part in range(1024 // CHUNK):
        rows = pl.ds(part * CHUNK, CHUNK)
        top = jnp.max(peak[rows, :], axis=1, keepdims=True)
        peak[rows, :] = jnp.broadcast_to(top, (CHUNK, 128))
    weigh(own_tile, True)
    each_before(weigh)

    column = lax.broadcasted_iota(jnp.int32, (128, 128), 1)
    logs = jnp.zeros((128, 128), jnp.float32)
    for h in range(8):
        rows = pl.ds(h * 128, 128)
        whole = jnp.sum(total[rows, :], axis=1, keepdims=True)
        attended = (weighed[rows, :] * (1.0 / whole)).astype(jnp.bfloat16)
        value = jnp.dot(attended, up_value[h], preferred_element_type=jnp.float32)
        values[h * 128 : h * 128 + 128, :] = jnp.transpose(value).astype(jnp.bfloat16)
        logs = jnp.where(column == h, peak[rows, :] * SCALE + jnp.log(whole), logs)
    log_sum[...] = jnp.transpose(logs)[0:8, :]


def third_kernel(place, own, right, left, low, high, *rest):
    out = rest[-1]
    for dx, array in ((0, own), (1, right), (3, left)):
        out[(place[0] + dx) & 3] = array[...]
    out[(place[0] + 2) & 3, 0:512] = low[...]
    out[(place[0] + 2) & 3, 512:1024] = high[...]


def project_kernel(wanted, place, mine, theirs, weights, outs):
    for chip in sorted({chip for chip, _ in wanted}):
        high, low = lax.div(place[1 + chip], 2), place[1 + chip] & 1
        right = jnp.concatenate(
            [mine[2 * low], theirs[2 * low], mine[2 * low + 1], theirs[2 * low + 1]], axis=1
        )
        halves = [half for other, half in wanted if other == chip]
        weight = weights[high, halves[0] : halves[-1] + 1].reshape(224 * len(halves), 1024)
        terms = jnp.dot(weight, right, preferred_element_type=jnp.float32).astype(jnp.bfloat16)
        for n, half in enumerate(halves):
            out = outs[wanted.index((chip, half))]
            for low_bit in range(2):
                out[low_bit] = terms[
                    n * 224 : n * 224 + 224, low_bit * 256 : low_bit * 256 + 256
                ]


def first_terms_kernel(place, mine, theirs, *rest):
    blocks, (far_give, left_give, weights, sems) = rest[:4], rest[4:]
    copies = []
    for dz in range(4):
        at = place[0] ^ dz
        copies.append((blocks[dz], weights.at[at & 1, 1 - (lax.div(at, 2) ^ place[5])]))
    copies = fetched(copies, sems)
    for copy in copies:
        copy.wait()
    project_kernel([(0, 0), (2, 0)], place, mine, theirs, weights, [far_give, left_give])


def other_terms_kernel(place, mine, theirs, weights, out):
    wanted = [(0, 1), (1, 0), (1, 1), (2, 1), (3, 0), (3, 1)]
    project_kernel(wanted, place, mine, theirs, weights, [out.at[n] for n in range(6)])


def summed(*arrays):
    whole = arrays[0][...].astype(jnp.float32)
    for array in arrays[1:]:
        whole = whole + array[...].astype(jnp.float32)
    return whole.astype(jnp.bfloat16)


def early_kernel(terms, far_give, left_give, out, far_out, part):
    part[...] = terms[4].astype(jnp.float32) + left_give[...].astype(jnp.float32)
    out[...] = summed(terms.at[1], far_give)
    far_out[...] = terms[0]


def give_kernel(place, terms, left, right, far_keep, *outs):
    same, cross, left_out, right_out, whole = outs
    whole[...] = summed(left, right)
    same[...] = whole[place[0]]
    cross[...] = whole[1 - place[0]]
    left_out[...] = summed(terms.at[3], far_keep)
    right_out[...] = terms[2]


def keep_kernel(place, terms, left, right, same, cross, whole):
    whole[...] = summed(terms.at[5], left, right)
    same[...] = whole[place[0]]
    cross[...] = whole[1 - place[0]]


def halves_kernel(give_same, give_cross, keep_same, keep_cross, mine, theirs):
    for cross, pair in enumerate(((keep_same, give_same), (keep_cross, give_cross))):
        whole = summed(*pair)
        mine[cross] = whole[:, 0:128]
        theirs[cross] = whole[:, 128:256]


def finish_kernel(place, mine, theirs, mixed, whole):
    for cross in range(2):
        for side, array in enumerate((mine, theirs)):
            whole[(place[0] ^ cross) * 2 + (place[1] ^ side)] = array[cross].astype(jnp.float32)
    mixed[...] = jnp.transpose(whole[...].reshape(896, 128)).astype(jnp.bfloat16)


def gather_ring(block):
    return [block] + [moved(block, along_x(-by)) for by in (1, 2, 3)]


def per_device(q_nope, q_rope, latent, rope_key, segment_ids, w_uk, w_uv, w_out):
    ctx, dp = lax.axis_index("ctx"), lax.axis_index("dp")
    z, x, core = ctx // 8, ctx // 2 % 4, ctx % 2
    half, y = dp // 4, dp % 4
    place = jnp.stack([z, x, core, ctx, segment_ids[0]]).astype(jnp.int32)
    docs = segment_ids.reshape(1, 128)

    tail = jnp.broadcast_to(docs.astype(jnp.bfloat16), (ROPE_DIM, 128))
    tail = jnp.concatenate([rope_key.T, tail])
    (block,) = call(
        keys_kernel,
        [((128, WIDE), jnp.bfloat16)],
        [HBM, VMEM],
        [pltpu.SemaphoreType.DMA((1,))],
        limit=8,
        name="keys",
    )(latent, tail)
    up = w_uk.reshape(8, 4, 4, 128).transpose(0, 2, 1, 3).reshape(8, 16, 128)
    up = jnp.concatenate([up, w_uv])
    ring = gather_ring(block)
    line = [up] + [moved(up, flip_z(bits)) for bits in (1, 2, 3)]
    row, line = call(
        first_kernel,
        [((4, 128, WIDE), jnp.bfloat16), ((4, 16, 16, 128), jnp.bfloat16)],
        [VMEM] * 8,
        limit=16,
        name="first",
    )(*ring, *line)
    plus, minus = moved(row, along_z_ring(-1)), moved(row, along_z_ring(1))
    low, high, twelve, ups = call(
        second_kernel,
        [
            ((2, 128, WIDE), jnp.bfloat16),
            ((2, 128, WIDE), jnp.bfloat16),
            ((12, 128, WIDE), jnp.bfloat16),
            ((4, 4, 16, 16, 128), jnp.bfloat16),
        ],
        [VMEM] * 7,
        limit=16,
        name="second",
    )(row, plus, minus, *gather_ring(line))
    pieces = [twelve, moved(low, along_z_ring(-1)), moved(high, along_z_ring(1))]
    theirs = moved(twelve, other_core)

    query, up_value, weight, token = call(
        queries_kernel,
        [
            ((1024, WIDE), jnp.bfloat16),
            ((8, KV_RANK, HEAD_DIM), jnp.bfloat16),
            ((224, 1024), jnp.bfloat16),
            ((8, 128), jnp.float32),
        ],
        [SMEM] + [HBM] * 3 + [VMEM] * 3,
        [
            pltpu.VMEM((8, HEAD_DIM, KV_RANK), jnp.bfloat16),
            pltpu.VMEM((128, 1024), jnp.bfloat16),
            pltpu.VMEM((128, 512), jnp.bfloat16),
            pltpu.SemaphoreType.DMA((3,)),
        ],
        limit=16,
        flops=700_000_000,
        name="queries",
    )(place, q_nope, q_rope, w_out.T, docs, ups, moved(ups, other_core))

    low, high = call(
        gate_kernel,
        [((2, 128, WIDE), jnp.bfloat16)] * 2,
        [VMEM] * 3,
        limit=8,
        name="gate",
    )(*pieces[1:], token)
    weights = [weight] + [moved(weight, flip_z(bits)) for bits in (1, 2, 3)]
    pieces = [twelve, low, high, theirs, moved(low, other_core), moved(high, other_core)]
    values, log_sum = call(
        attention_kernel,
        [((1024, 128), jnp.bfloat16), ((8, 128), jnp.float32)],
        [SMEM] + [VMEM] * 8,
        [
            pltpu.VMEM((4096, WIDE), jnp.bfloat16),
            pltpu.VMEM((4096 // TILE, 1024, TILE), jnp.float32),
            pltpu.VMEM((1024, 128), jnp.float32),
            pltpu.VMEM((1024, 128), jnp.float32),
            pltpu.VMEM((1024, KV_RANK), jnp.float32),
        ],
        limit=32,
        flops=10_000_000_000,
        name="attention",
    )(place, query, up_value, *pieces)

    (values,) = call(
        hold_kernel, [((1024, 128), jnp.bfloat16)], [VMEM] * 2, limit=8, name="hold"
    )(values, weights[1])
    right, left = moved(values, along_x(-1)), moved(values, along_x(1))
    low, high = call(
        outer_kernel, [((512, 128), jnp.bfloat16)] * 2, [VMEM] * 2, limit=8, name="outer"
    )(right, left)
    low, high = moved(low, along_x(-1)), moved(high, along_x(1))
    (gathered,) = call(
        third_kernel, [((4, 1024, 128), jnp.bfloat16)], [SMEM] + [VMEM] * 7, limit=8, name="third"
    )(x.reshape(1).astype(jnp.int32), values, right, left, low, high, *weights[2:])
    order = jnp.stack([z, (y + 2) % 4, (y + 1) % 4, (y + 3) % 4, y, half]).astype(jnp.int32)
    theirs = moved(gathered, other_core)
    term, pair = ((2, 224, 256), jnp.bfloat16), [((224, 256), jnp.bfloat16)] * 2
    far_give, left_give, held = call(
        first_terms_kernel,
        [term] * 2 + [((2, 2, 224, 1024), jnp.bfloat16)],
        [SMEM] + [VMEM] * 2 + [ANY] * 4,
        [pltpu.SemaphoreType.DMA((4,))],
        limit=16,
        flops=470_000_000,
        name="project",
    )(order, gathered, theirs, *weights)
    (terms,) = call(
        other_terms_kernel,
        [((6, 2, 224, 256), jnp.bfloat16)],
        [SMEM] + [VMEM] * 3,
        limit=16,
        flops=1_410_000_000,
        name="others",
    )(order, gathered, theirs, held)
    low = jnp.stack([x % 2, core]).astype(jnp.int32)
    left_give = moved(left_give, along_y(-1))
    right_give, far_keep, left_give = call(
        early_kernel, [term] * 2 + [((2, 224, 256), jnp.float32)], [VMEM] * 3, limit=16, name="early"
    )(terms, moved(far_give, along_y(1)), left_give)
    same, cross, left_keep, right_keep = call(
        give_kernel,
        pair + [term] * 2,
        [SMEM] + [VMEM] * 4,
        [pltpu.VMEM((2, 224, 256), jnp.bfloat16)],
        limit=16,
        name="give",
    )(low, terms, moved(right_give, along_y(1)), left_give, moved(far_keep, along_y(-1)))
    give = [moved(same, settle(False, True)), moved(cross, settle(True, True))]
    same, cross = call(
        keep_kernel,
        pair,
        [SMEM] + [VMEM] * 3,
        [pltpu.VMEM((2, 224, 256), jnp.bfloat16)],
        limit=16,
        name="keep",
    )(low, terms, moved(right_keep, along_y(1)), moved(left_keep, along_y(-1)))
    keep = [moved(same, settle(False, False)), moved(cross, settle(True, False))]
    mine, theirs = call(
        halves_kernel, [((2, 224, 128), jnp.bfloat16)] * 2, [VMEM] * 4, limit=16, name="halves"
    )(*give, *keep)
    (mixed,) = call(
        finish_kernel,
        [((128, 896), jnp.bfloat16)],
        [SMEM] + [VMEM] * 2,
        [pltpu.VMEM((4, 224, 128), jnp.float32)],
        limit=16,
        name="finish",
    )(low, mine, moved(theirs, other_core))
    return (mixed, log_sum.T)


def solution(mesh):
    return jax.shard_map(
        per_device,
        mesh=mesh,
        in_specs=(
            P("ctx", "dp"),
            P("ctx", "dp"),
            P("ctx", None),
            P("ctx", None),
            P("ctx"),
            P("dp", "ctx", None),
            P("dp", "ctx", None),
            P("dp", "ctx"),
        ),
        out_specs=(P("ctx", "dp"), P("ctx", "dp")),
        check_vma=False,
    )
```
